32 devices in a mesh: gx: 8 (over y, x, core), gy: 4 (over z).
Axes of the slice: x: 2, y: 2, z: 4, core: 2. Of those that a mesh axis runs over, the one named last changes fastest.
Arguments:
- hidden_in: bfloat16 [256, 16384], P(('gx', 'gy')), may hold values from -6 to 6
- norm_gain: float32 [16384], replicated, may hold values from 0.1 to 1.9
- w_qkv: bfloat16 [16384, 18432], P('gy', 'gx'), may hold values from -0.046875 to 0.046875
- k_cache: bfloat16 [256, 512, 1024], P(('gx', 'gy')), may hold values from -60 to 60
- v_cache: bfloat16 [256, 512, 1024], P(('gx', 'gy')), may hold values from -6 to 6
- lengths: int32 [256], P(('gx', 'gy')), may hold values from 1 to 512, as said below
- w_out: bfloat16 [16384, 16384], P('gy', 'gx'), may hold values from -0.375 to 0.375
Outputs:
- attn_out: bfloat16 [256, 16384], P(('gx', 'gy'))
The draws below stay inside these ranges and needn't reach their ends.
Inputs may be any that keep to these rules, and one draw needn't show every extreme that they name: Row b attends to its first lengths[b] cached positions; some row has 512.
All inputs are finite; a program needn't handle non-finite values.
Results may differ from the reference program's by a relative error of at most 0.015.
The reference program's roundings to bfloat16 on the way count: a program that leaves them out, or rounds other values in their place, can miss the bound.
Values may be sent and summed in bfloat16 or wider, within the bound.
No kernel may reach another device: no remote copies, remote signals or barrier semaphores. Data moves between devices by JAX's collectives and lax.ppermute only.
A program may use at most 128 MiB of HBM per device.

```python
import math
import jax
import jax.numpy as jnp
from jax import lax

D = 16384
HQ = 128
KVH = 8
HD = 128
ROWS_DEV = 8
CACHE = 512
BATCH = 256
ATT = 16384
QCOLS = 18432


def draw_lengths(key, part):
    key = jax.random.fold_in(key, 11)
    first, second, third = jax.random.split(key, 3)
    base = jax.random.randint(first, (BATCH,), 1, CACHE + 1)
    factor = jax.random.randint(second, (BATCH // ROWS_DEV,), 1, 5)
    factor = jnp.repeat(factor, ROWS_DEV)
    lengths = jnp.maximum(base // factor, 1)
    chosen = jax.random.randint(third, (), 0, BATCH)
    return jnp.where(jnp.arange(BATCH) == chosen, CACHE, lengths).astype(jnp.int32)


def draw_k_cache(key, part):
    key = jax.random.fold_in(key, 5)
    first = jax.random.fold_in(key, 0)
    values = jax.random.truncated_normal(first, -6.0, 6.0, (BATCH, CACHE, KVH * HD), jnp.float32)
    return values.astype(jnp.bfloat16)


def steps_of(stream_key, shape, cuts, least, largest):
    loudness = 1.0
    for axis_at, parts in cuts:
        draws = jax.random.uniform(jax.random.fold_in(jax.random.fold_in(stream_key, 6), axis_at), (parts,), jnp.float32, least / len(cuts), largest / len(cuts))
        loudness = loudness * jnp.repeat(jnp.exp(draws), shape[axis_at] // parts).reshape((-1,) + (1,) * (len(shape) - 1 - axis_at))
    return loudness


def bell_draw(stream_key, shape, scale, limit, cuts=(), kind=jnp.bfloat16):
    result = scale * jax.random.normal(stream_key, shape, jnp.float32)
    if cuts:
        result = result * steps_of(stream_key, shape, cuts, -0.22, 0.18)
    return jnp.clip(result, -limit, limit).astype(kind)


def setup_inputs(seed: int = 0) -> dict:
    streams_of = jax.random.split(jax.random.key(seed), 8)
    return {
        "hidden_in": bell_draw(streams_of[0], (BATCH, D), 1.0, 6.0, ((0, 32),)),
        "norm_gain": jnp.clip(1.0 + 0.18 * jax.random.normal(streams_of[1], (D,), jnp.float32), 0.1, 1.9),
        "w_qkv": bell_draw(streams_of[2], (D, QCOLS), D ** -0.5, 0.046875, ((0, 4), (1, 8))),
        "k_cache": draw_k_cache(jax.random.fold_in(streams_of[7], 71), 0),
        "v_cache": bell_draw(streams_of[4], (BATCH, CACHE, KVH * HD), 1.0, 6.0, ((0, 32),)),
        "lengths": draw_lengths(jax.random.fold_in(streams_of[7], 71), 0),
        "w_out": bell_draw(streams_of[6], (ATT, D), (ATT // 64) ** -0.5, 0.375, ((0, 4), (1, 8))),
    }


eps = 1e-05
theta = 500000.0

def rotate(values, position, head_size):
    half = head_size // 2
    index = jnp.arange(half, dtype=jnp.float32)
    freqs = theta ** (-2.0 * index / head_size)
    angle = position[:, None, None] * freqs[None, None, :]
    cosine = jnp.cos(angle)
    sine = jnp.sin(angle)
    first = values[..., :half]
    second = values[..., half:]
    return jnp.concatenate([first * cosine - second * sine, second * cosine + first * sine], axis=-1)

def attend_rows(qkv, k_cache, v_cache, lengths):
    rows = qkv.shape[0]
    span = k_cache.shape[1]
    share = HQ // KVH
    query = qkv[:, :HQ * HD].reshape(rows, HQ, HD).astype(jnp.float32)
    key_new = qkv[:, HQ * HD:(HQ + KVH) * HD].reshape(rows, KVH, HD).astype(jnp.float32)
    value_new = qkv[:, (HQ + KVH) * HD:].reshape(rows, KVH, HD).astype(jnp.float32)
    position = lengths.astype(jnp.float32)
    query = rotate(query, position, HD).astype(jnp.bfloat16).astype(jnp.float32)
    key_new = rotate(key_new, position, HD).astype(jnp.bfloat16).astype(jnp.float32)
    grouped = query.reshape(rows, KVH, share, HD)
    keys = k_cache.reshape(rows, span, KVH, HD).astype(jnp.float32)
    values = v_cache.reshape(rows, span, KVH, HD).astype(jnp.float32)
    scale = 1.0 / math.sqrt(HD)
    scores = jnp.einsum('rgsd,rtgd->rgst', grouped, keys) * scale
    fresh = jnp.einsum('rgsd,rgd->rgs', grouped, key_new) * scale
    valid = jnp.arange(span, dtype=jnp.int32)[None, :] < lengths[:, None]
    scores = jnp.where(valid[:, None, None, :], scores, -jnp.inf)
    top = jnp.maximum(lax.optimization_barrier(jnp.max(scores, axis=-1)), fresh)
    probs = jnp.exp(scores - top[..., None])
    pnew = jnp.exp(fresh - top)
    total = lax.optimization_barrier(jnp.sum(probs, axis=-1)) + pnew
    weights = (probs / total[..., None]).astype(jnp.bfloat16).astype(jnp.float32)
    wnew = (pnew / total).astype(jnp.bfloat16).astype(jnp.float32)
    mixed = jnp.einsum('rgst,rtgd->rgsd', weights, values) + wnew[..., None] * value_new[:, :, None, :]
    return mixed.reshape(rows, HQ * HD).astype(jnp.bfloat16)

def reference(hidden_in, norm_gain, w_qkv, k_cache, v_cache, lengths, w_out):
    widened = hidden_in.astype(jnp.float32)
    normed = (widened * lax.rsqrt(lax.optimization_barrier(jnp.mean(widened * widened, axis=-1, keepdims=True)) + eps) * norm_gain).astype(jnp.bfloat16)
    qkv = jnp.dot(normed, w_qkv, preferred_element_type=jnp.float32).astype(jnp.bfloat16)
    blocks = BATCH // ROWS_DEV
    pieces = (qkv.reshape(blocks, ROWS_DEV, QCOLS), k_cache.reshape(blocks, ROWS_DEV, CACHE, KVH * HD), v_cache.reshape(blocks, ROWS_DEV, CACHE, KVH * HD), lengths.reshape(blocks, ROWS_DEV))
    attended = lax.map(lambda p: attend_rows(p[0], p[1], p[2], p[3]), pieces).reshape(BATCH, HQ * HD)
    return jnp.dot(attended, w_out, preferred_element_type=jnp.float32).astype(jnp.bfloat16)
```

```python
import math

import jax
import jax.numpy as jnp
from jax import lax
from jax.experimental import pallas as pl
from jax.experimental.pallas import tpu as pltpu
from jax.sharding import PartitionSpec as P

HQ = 128
KVH = 8
HD = 128


eps = 1e-05
theta = 500000.0
ROOM = 50 * 2**20


def rotate(values, position, head_size):
    half = head_size // 2
    index = jnp.arange(half, dtype=jnp.float32)
    freqs = theta ** (-2.0 * index / head_size)
    angle = position[:, None, None] * freqs[None, None, :]
    cosine = jnp.cos(angle)
    sine = jnp.sin(angle)
    first = values[..., :half]
    second = values[..., half:]
    return jnp.concatenate(
        [first * cosine - second * sine, second * cosine + first * sine], axis=-1
    )


PART = 128


def attend_kernel(lengths, query, key_new, value_new, k_cache, v_cache, out, keys, values, wide, sems):
    rows, span = keys.shape[:2]
    share = HQ // KVH
    parts = span // PART
    scale = 1.0 / math.sqrt(HD)

    def copies(row, part):
        some = pl.ds(part * PART, PART)
        return (
            pltpu.make_async_copy(
                k_cache.at[row, some], keys.at[row, some], sems.at[row, part, 0]
            ),
            pltpu.make_async_copy(
                v_cache.at[row, some], values.at[row, some], sems.at[row, part, 1]
            ),
        )

    for row in range(rows):
        for part in range(parts):

            @pl.when(part * PART < lengths[row])
            def _():
                for copy in copies(row, part):
                    copy.start()

    wide[...] = jnp.zeros_like(wide)

    def one_row(row, used):
        count = used * PART
        for part in range(used):
            for copy in copies(row, part):
                copy.wait()
        for group in range(KVH):
            heads = pl.ds(group * share, share)
            wide[heads, group * HD : (group + 1) * HD] = query[row, heads]
        scores = lax.dot_general(
            wide[...],
            keys[row, :count],
            (((1,), (1,)), ((), ())),
            preferred_element_type=jnp.float32,
        )
        position = lax.broadcasted_iota(jnp.int32, scores.shape, 1)
        scores = jnp.where(position < lengths[row], scores * scale, -jnp.inf)
        fresh_key = jnp.broadcast_to(key_new[row][:, None, :], (KVH, share, HD))
        fresh_key = fresh_key.reshape(HQ, HD).astype(jnp.float32)
        fresh = jnp.sum(query[row].astype(jnp.float32) * fresh_key, axis=1, keepdims=True) * scale
        top = jnp.maximum(jnp.max(scores, axis=1, keepdims=True), fresh)
        probs = jnp.exp(scores - top)
        pnew = jnp.exp(fresh - top)
        unit = 1.0 / (jnp.sum(probs, axis=1, keepdims=True) + pnew)
        weights = (probs * unit).astype(jnp.bfloat16)
        wnew = (pnew * unit).astype(jnp.bfloat16).astype(jnp.float32)
        mixed = jnp.dot(weights, values[row, :count], preferred_element_type=jnp.float32)
        for group in range(KVH):
            heads = slice(group * share, (group + 1) * share)
            own = mixed[heads, group * HD : (group + 1) * HD]
            own = own + wnew[heads] * value_new[row, group : group + 1]
            out[row, heads] = own.astype(out.dtype)

    @pl.loop(0, rows)
    def _(row):
        used = (lengths[row] + PART - 1) // PART
        for case in range(1, parts + 1):

            @pl.when(used == case)
            def _():
                one_row(row, case)


def attend_local(owned, k_cache, v_cache, lengths):
    rows = owned.shape[0]
    query = owned[:, : HQ * HD].reshape(rows, HQ, HD).astype(jnp.float32)
    key_new = owned[:, HQ * HD : (HQ + KVH) * HD].reshape(rows, KVH, HD).astype(jnp.float32)
    value_new = owned[:, (HQ + KVH) * HD :].reshape(rows, KVH, HD).astype(jnp.float32)
    position = lengths.astype(jnp.float32)
    query = rotate(query, position, HD).astype(jnp.bfloat16)
    key_new = rotate(key_new, position, HD).astype(jnp.bfloat16)
    span, width = k_cache.shape[1:]
    vmem = pl.BlockSpec(memory_space=pltpu.VMEM)
    anywhere = pl.BlockSpec(memory_space=pl.ANY)
    mixed = pl.pallas_call(
        attend_kernel,
        in_specs=[
            pl.BlockSpec(memory_space=pltpu.SMEM),
            vmem,
            vmem,
            vmem,
            anywhere,
            anywhere,
        ],
        out_specs=vmem,
        out_shape=jax.ShapeDtypeStruct((rows, HQ, HD), jnp.bfloat16),
        scratch_shapes=[
            pltpu.VMEM((rows, span, width), jnp.bfloat16),
            pltpu.VMEM((rows, span, width), jnp.bfloat16),
            pltpu.VMEM((HQ, width), jnp.bfloat16),
            pltpu.SemaphoreType.DMA((rows, span // PART, 2)),
        ],
        compiler_params=pltpu.CompilerParams(vmem_limit_bytes=ROOM),
        cost_estimate=pl.CostEstimate(
            flops=4 * rows * span * width * HQ,
            bytes_accessed=2 * rows * span * width,
            transcendentals=rows * span * HQ,
        ),
    )(lengths, query, key_new, value_new, k_cache, v_cache)
    return mixed.reshape(rows, HQ * HD)


def swap(block, axis, bit):
    count = lax.axis_size(axis)
    return lax.ppermute(block, axis, [(i, i ^ bit) for i in range(count)])


def all_rows(block):
    if lax.axis_size("gx") != 8:
        pieces = lax.all_gather(block, "gx", axis=0)
        count, rows, width = pieces.shape
        return pieces.reshape(count, 2, rows // 2, width).transpose(1, 0, 2, 3)
    mine = [block] + [swap(block, "gx", chip) for chip in (2, 4, 6)]
    theirs = [swap(piece, "gx", 1) for piece in mine]
    pieces = [piece for pair in zip(mine, theirs) for piece in pair]
    halves = [piece.reshape(2, 1, -1, block.shape[1]) for piece in pieces]
    return jnp.concatenate(halves, axis=1)


def multiply_kernel(rows_ref, weights_ref, out_ref):
    out_ref[...] = jnp.dot(
        rows_ref[...], weights_ref[...], preferred_element_type=jnp.float32
    )


def multiply(rows, weights):
    count, depth = rows.shape
    columns = weights.shape[1]
    tile = 256 if columns % 256 == 0 else columns
    return pl.pallas_call(
        multiply_kernel,
        grid=(columns // tile,),
        in_specs=[
            pl.BlockSpec(memory_space=pltpu.VMEM),
            pl.BlockSpec((depth, tile), lambda j: (0, j)),
        ],
        out_specs=pl.BlockSpec((count, tile), lambda j: (0, j)),
        out_shape=jax.ShapeDtypeStruct((count, columns), jnp.float32),
        compiler_params=pltpu.CompilerParams(vmem_limit_bytes=ROOM),
        cost_estimate=pl.CostEstimate(
            flops=2 * count * depth * columns,
            bytes_accessed=2 * depth * columns,
            transcendentals=0,
        ),
    )(rows, weights)


def project(rows, weights, scale):
    width = weights.shape[0]
    here = lax.axis_index("gy")

    def features(owner):
        return lax.dynamic_slice_in_dim(rows, owner * width, width, axis=1)

    def send(values, bit):
        packed = (values * scale).astype(jnp.float16)
        return swap(packed, "gy", bit).astype(jnp.float32) * (1.0 / scale)

    far = jnp.concatenate([swap(features(here ^ bit), "gy", bit) for bit in (2, 3)])
    near, far = lax.optimization_barrier((features(here ^ 1), far))
    near = jnp.concatenate([features(here), swap(near, "gy", 1)])
    far = all_rows(far)
    near = all_rows(near)
    shape = far.shape[:3] + weights.shape[1:]
    far = multiply(far.reshape(-1, width), weights).reshape(shape)
    pair = far[0] + send(far[1], 1)
    near = multiply(near.reshape(-1, width), weights).reshape(shape)
    return near[0] + send(near[1], 1) + send(pair, 2)


def deliver(columns):
    count, rows, width = columns.shape
    if count != 8:
        owned = lax.all_to_all(columns, "gx", split_axis=0, concat_axis=0)
    else:
        pairs = [columns[:2]] + [
            swap(columns[chip : chip + 2], "gx", chip) for chip in (2, 4, 6)
        ]
        theirs = swap(jnp.stack([pair[1] for pair in pairs]), "gx", 1)
        owned = jnp.stack([pair[0] for pair in pairs])
        owned = jnp.stack([owned, theirs], axis=1).reshape(count, rows, width)
        owned = owned[jnp.arange(count) ^ lax.axis_index("gx")]
    return owned.transpose(1, 0, 2).reshape(rows, count * width)


def level(rows):
    rows = rows.astype(jnp.float32)
    top = jnp.max(jnp.abs(rows), axis=-1, keepdims=True)
    scale = jnp.ones_like(top)
    unit = jnp.ones_like(top)
    for power in (64, 32, 16, 8, 4, 2, 1):
        large = top * scale > 2.0 ** (power - 1)
        scale = jnp.where(large, scale * 2.0**-power, scale)
        unit = jnp.where(large, unit * 2.0**power, unit)
    for power in (64, 32, 16, 8, 4, 2, 1):
        small = top * scale <= 2.0**-power
        scale = jnp.where(small, scale * 2.0**power, scale)
        unit = jnp.where(small, unit * 2.0**-power, unit)
    return (rows * scale).astype(jnp.bfloat16), unit


def on_device(hidden_in, norm_gain, w_qkv, k_cache, v_cache, lengths, w_out):
    widened = hidden_in.astype(jnp.float32)
    normed = (
        widened * lax.rsqrt(jnp.mean(widened * widened, axis=-1, keepdims=True) + eps) * norm_gain
    ).astype(jnp.bfloat16)
    qkv = project(normed, w_qkv, 32.0)
    owned = deliver(qkv.astype(jnp.bfloat16))
    attended = attend_local(owned, k_cache, v_cache, lengths)
    scaled, unit = level(attended)
    out = deliver(project(scaled, w_out, 8.0).astype(jnp.bfloat16))
    return (out.astype(jnp.float32) * unit).astype(jnp.bfloat16)


def solution(mesh):
    return jax.shard_map(
        on_device,
        mesh=mesh,
        in_specs=(
            P(("gx", "gy"), None),
            P(),
            P("gy", "gx"),
            P(("gx", "gy"), None, None),
            P(("gx", "gy"), None, None),
            P(("gx", "gy")),
            P("gy", "gx"),
        ),
        out_specs=P(("gx", "gy"), None),
        check_vma=False,
    )
```

```python
import functools
import math

import jax
import jax.numpy as jnp
from jax import lax
from jax.experimental import pallas as pl
from jax.experimental.pallas import tpu as pltpu
from jax.sharding import PartitionSpec as P

HQ = 128
KVH = 8
HD = 128


eps = 1e-05
theta = 500000.0
ROOM = 50 * 2**20


def rotate(values, position, head_size):
    half = head_size // 2
    index = jnp.arange(half, dtype=jnp.float32)
    freqs = theta ** (-2.0 * index / head_size)
    angle = position[:, None, None] * freqs[None, None, :]
    cosine = jnp.cos(angle)
    sine = jnp.sin(angle)
    first = values[..., :half]
    second = values[..., half:]
    return jnp.concatenate(
        [first * cosine - second * sine, second * cosine + first * sine], axis=-1
    )


PART = 128
GROUP = 4


def attend_kernel(lengths, query, key_new, value_new, k_cache, v_cache, out, keys, values, wide, sems):
    rows, span = keys.shape[:2]
    share = HQ // KVH
    parts = span // PART
    scale = 1.0 / math.sqrt(HD)

    def copies(row, count):
        some = pl.ds(0, count)
        return (
            pltpu.make_async_copy(k_cache.at[row, some], keys.at[row, some], sems.at[row, 0]),
            pltpu.make_async_copy(v_cache.at[row, some], values.at[row, some], sems.at[row, 1]),
        )

    def by_length(length, act):
        for case in range(1, parts + 1):
            pl.when((length + PART - 1) // PART == case)(functools.partial(act, case * PART))

    def fetch(row, count):
        for copy in copies(row, count):
            copy.start()

    def arrive(row, count):
        for copy in copies(row, count):
            copy.wait()

    def clear(row, part):
        values[row, part * PART : (part + 1) * PART] = jnp.zeros(
            (PART, values.shape[2]), values.dtype
        )

    def score(row, wide, count):
        for group in range(KVH):
            heads = pl.ds(group * share, share)
            wide[heads, group * HD : (group + 1) * HD] = query[row, heads]
        scores = lax.dot_general(
            wide[...],
            keys[row, :count],
            (((1,), (1,)), ((), ())),
            preferred_element_type=jnp.float32,
        )
        position = lax.broadcasted_iota(jnp.int32, scores.shape, 1)
        return jnp.where(position < lengths[row], scores * scale, -jnp.inf)

    def weigh(row, scores):
        fresh_key = jnp.broadcast_to(key_new[row][:, None, :], (KVH, share, HD))
        fresh_key = fresh_key.reshape(HQ, HD).astype(jnp.float32)
        fresh = jnp.sum(query[row].astype(jnp.float32) * fresh_key, axis=1, keepdims=True) * scale
        top = jnp.maximum(jnp.max(scores, axis=1, keepdims=True), fresh)
        probs = jnp.exp(scores - top)
        pnew = jnp.exp(fresh - top)
        unit = 1.0 / (jnp.sum(probs, axis=1, keepdims=True) + pnew)
        weights = (probs * unit).astype(jnp.bfloat16)
        return weights, (pnew * unit).astype(jnp.bfloat16).astype(jnp.float32)

    def mix(row, weights, wnew, count):
        mixed = jnp.dot(weights, values[row, :count], preferred_element_type=jnp.float32)
        for group in range(KVH):
            heads = slice(group * share, (group + 1) * share)
            own = mixed[heads, group * HD : (group + 1) * HD]
            own = own + wnew[heads] * value_new[row, group : group + 1]
            out[row, heads] = own.astype(out.dtype)

    def group(row, count):
        each = [row + at for at in range(GROUP)]
        for one in each:
            by_length(lengths[one], functools.partial(arrive, one))
            for part in range(1, count // PART):
                pl.when(lengths[one] <= part * PART)(functools.partial(clear, one, part))
        scores = [score(one, wide.at[at], count) for at, one in enumerate(each)]
        weighed = [weigh(one, of_one) for one, of_one in zip(each, scores)]
        for one, (weights, wnew) in zip(each, weighed):
            mix(one, weights, wnew, count)

    @pl.loop(0, rows)
    def _(row):
        by_length(lengths[row], functools.partial(fetch, row))

    wide[...] = jnp.zeros_like(wide)

    @pl.loop(0, rows // GROUP)
    def _(index):
        row = index * GROUP
        longest = lengths[row]
        for at in range(1, GROUP):
            longest = jnp.maximum(longest, lengths[row + at])
        by_length(longest, functools.partial(group, row))


def attend_local(owned, k_cache, v_cache, lengths):
    rows = owned.shape[0]
    query = owned[:, : HQ * HD].reshape(rows, HQ, HD).astype(jnp.float32)
    key_new = owned[:, HQ * HD : (HQ + KVH) * HD].reshape(rows, KVH, HD).astype(jnp.float32)
    value_new = owned[:, (HQ + KVH) * HD :].reshape(rows, KVH, HD).astype(jnp.float32)
    position = lengths.astype(jnp.float32)
    query = rotate(query, position, HD).astype(jnp.bfloat16)
    key_new = rotate(key_new, position, HD).astype(jnp.bfloat16)
    span, width = k_cache.shape[1:]
    vmem = pl.BlockSpec(memory_space=pltpu.VMEM)
    anywhere = pl.BlockSpec(memory_space=pl.ANY)
    mixed = pl.pallas_call(
        attend_kernel,
        in_specs=[
            pl.BlockSpec(memory_space=pltpu.SMEM),
            vmem,
            vmem,
            vmem,
            anywhere,
            anywhere,
        ],
        out_specs=vmem,
        out_shape=jax.ShapeDtypeStruct((rows, HQ, HD), jnp.bfloat16),
        scratch_shapes=[
            pltpu.VMEM((rows, span, width), jnp.bfloat16),
            pltpu.VMEM((rows, span, width), jnp.bfloat16),
            pltpu.VMEM((GROUP, HQ, width), jnp.bfloat16),
            pltpu.SemaphoreType.DMA((rows, 2)),
        ],
        compiler_params=pltpu.CompilerParams(vmem_limit_bytes=ROOM),
        cost_estimate=pl.CostEstimate(
            flops=4 * rows * span * width * HQ,
            bytes_accessed=2 * rows * span * width,
            transcendentals=rows * span * HQ,
        ),
    )(lengths, query, key_new, value_new, k_cache, v_cache)
    return mixed.reshape(rows, HQ * HD)


def swap(block, axis, bit):
    count = lax.axis_size(axis)
    return lax.ppermute(block, axis, [(i, i ^ bit) for i in range(count)])


def all_rows(block):
    if lax.axis_size("gx") != 8:
        pieces = lax.all_gather(block, "gx", axis=0)
        count, rows, width = pieces.shape
        return pieces.reshape(count, 2, rows // 2, width).transpose(1, 0, 2, 3)
    mine = [block] + [swap(block, "gx", chip) for chip in (2, 4, 6)]
    theirs = [swap(piece, "gx", 1) for piece in mine]
    pieces = [piece for pair in zip(mine, theirs) for piece in pair]
    halves = [piece.reshape(2, 1, -1, block.shape[1]) for piece in pieces]
    return jnp.concatenate(halves, axis=1)


def multiply_kernel(start, far, near, weights, out, held, sems):
    parts, depth, columns = held.shape

    def copy(part):
        return pltpu.make_async_copy(
            weights.at[pl.ds(part * depth, depth), pl.ds(start, columns)],
            held.at[part],
            sems.at[part],
        )

    for part in range(parts):
        copy(part).start()
    out[...] = jnp.zeros_like(out)

    @pl.loop(0, parts)
    def _(part):
        copy(part).wait()
        some = pl.ds(pl.multiple_of(part * depth, depth), depth)
        rows = jnp.concatenate([far[:, some], near[:, some]], axis=0)
        out[...] += jnp.dot(rows, held[part], preferred_element_type=jnp.float32)


def multiply(far, near, weights, start, columns):
    half, width = far.shape
    depth = 512
    vmem = pl.BlockSpec(memory_space=pltpu.VMEM)
    return pl.pallas_call(
        functools.partial(multiply_kernel, start),
        in_specs=[vmem, vmem, pl.BlockSpec(memory_space=pl.ANY)],
        out_specs=vmem,
        out_shape=jax.ShapeDtypeStruct((2 * half, columns), jnp.float32),
        scratch_shapes=[
            pltpu.VMEM((width // depth, depth, columns), jnp.bfloat16),
            pltpu.SemaphoreType.DMA((width // depth,)),
        ],
        compiler_params=pltpu.CompilerParams(vmem_limit_bytes=ROOM),
        cost_estimate=pl.CostEstimate(
            flops=4 * half * width * columns,
            bytes_accessed=2 * width * columns,
            transcendentals=0,
        ),
    )(far, near, weights)


def project(rows, weights, scale):
    width, columns = weights.shape
    here = lax.axis_index("gy")

    def features(owner):
        return lax.dynamic_slice_in_dim(rows, owner * width, width, axis=1)

    def pack(values):
        return (values * scale).astype(jnp.float16)

    def send(packed, bit):
        return swap(packed, "gy", bit).astype(jnp.float32) * (1.0 / scale)

    near, far, last = (swap(features(here ^ bit), "gy", bit) for bit in (1, 2, 3))
    near = jnp.concatenate([features(here), near])
    far = all_rows(jnp.concatenate([far, last]))
    near = all_rows(near)
    shape = (2, 2) + far.shape[1:3]
    far = far.reshape(-1, width)
    near = near.reshape(-1, width)
    first = columns // 512 * 256 if columns % 256 == 0 else columns
    left = multiply(far, near, weights, 0, first).reshape(shape + (first,))
    go_left = pack(left[:, 1])
    go_left, far, near = lax.optimization_barrier((go_left, far, near))
    left = left[:, 0] + send(go_left, 1)
    if first == columns:
        return [left[1] + send(pack(left[0]), 2)]
    right = multiply(far, near, weights, first, columns - first)
    right = right.reshape(shape + (columns - first,))
    go_far = pack(right[0, 1])
    across, go_near = lax.optimization_barrier((pack(left[0]), pack(right[1, 1])))
    left = left[1] + send(across, 2)
    across = pack(right[0, 0] + send(go_far, 1))
    right = right[1, 0] + send(go_near, 1) + send(across, 2)
    return [left, right]


def collect(columns):
    columns = columns.astype(jnp.bfloat16)
    count, rows, width = columns.shape
    if count != 8:
        return lax.all_to_all(columns, "gx", split_axis=0, concat_axis=0)
    pairs = [columns[:2]] + [
        swap(columns[chip : chip + 2], "gx", chip) for chip in (2, 4, 6)
    ]
    theirs = swap(jnp.stack([pair[1] for pair in pairs]), "gx", 1)
    owned = jnp.stack([pair[0] for pair in pairs])
    return jnp.stack([owned, theirs], axis=1).reshape(count, rows, width)


def deliver(parts):
    owned = jnp.concatenate([collect(part) for part in parts], axis=-1)
    count, rows, width = owned.shape
    if count == 8:
        owned = owned[jnp.arange(count) ^ lax.axis_index("gx")]
    return owned.transpose(1, 0, 2).reshape(rows, count * width)


def level(rows):
    rows = rows.astype(jnp.float32)
    top = jnp.max(jnp.abs(rows), axis=-1, keepdims=True)
    scale = jnp.ones_like(top)
    unit = jnp.ones_like(top)
    for power in (64, 32, 16, 8, 4, 2, 1):
        large = top * scale > 2.0 ** (power - 1)
        scale = jnp.where(large, scale * 2.0**-power, scale)
        unit = jnp.where(large, unit * 2.0**power, unit)
    for power in (64, 32, 16, 8, 4, 2, 1):
        small = top * scale <= 2.0**-power
        scale = jnp.where(small, scale * 2.0**power, scale)
        unit = jnp.where(small, unit * 2.0**-power, unit)
    return (rows * scale).astype(jnp.bfloat16), unit


def on_device(hidden_in, norm_gain, w_qkv, k_cache, v_cache, lengths, w_out):
    widened = hidden_in.astype(jnp.float32)
    normed = (
        widened * lax.rsqrt(jnp.mean(widened * widened, axis=-1, keepdims=True) + eps) * norm_gain
    ).astype(jnp.bfloat16)
    qkv = project(normed, w_qkv, 32.0)
    owned = deliver(qkv)
    attended = attend_local(owned, k_cache, v_cache, lengths)
    scaled, unit = level(attended)
    out = deliver(project(scaled, w_out, 8.0))
    return (out.astype(jnp.float32) * unit).astype(jnp.bfloat16)


def solution(mesh):
    return jax.shard_map(
        on_device,
        mesh=mesh,
        in_specs=(
            P(("gx", "gy"), None),
            P(),
            P("gy", "gx"),
            P(("gx", "gy"), None, None),
            P(("gx", "gy"), None, None),
            P(("gx", "gy")),
            P("gy", "gx"),
        ),
        out_specs=P(("gx", "gy"), None),
        check_vma=False,
    )
```

```python
import functools
import math

import jax
import jax.numpy as jnp
from jax import lax
from jax.experimental import pallas as pl
from jax.experimental.pallas import tpu as pltpu
from jax.sharding import PartitionSpec as P

HQ = 128
KVH = 8
HD = 128


eps = 1e-05
theta = 500000.0
ROOM = 50 * 2**20


def rotate(values, position, head_size):
    half = head_size // 2
    index = jnp.arange(half, dtype=jnp.float32)
    freqs = theta ** (-2.0 * index / head_size)
    angle = position[:, None, None] * freqs[None, None, :]
    cosine = jnp.cos(angle)
    sine = jnp.sin(angle)
    first = values[..., :half]
    second = values[..., half:]
    return jnp.concatenate(
        [first * cosine - second * sine, second * cosine + first * sine], axis=-1
    )


PART = 128
GROUP = 4


def attend_kernel(lengths, query, key_new, value_new, k_cache, v_cache, out, keys, values, wide, sems):
    rows, span = keys.shape[:2]
    share = HQ // KVH
    parts = span // PART
    scale = 1.0 / math.sqrt(HD)

    def copy(cache, row, count):
        source, target = ((k_cache, keys), (v_cache, values))[cache]
        some = pl.ds(0, count)
        return pltpu.make_async_copy(
            source.at[row, some], target.at[row, some], sems.at[row, cache]
        )

    def by_length(length, act):
        for case in range(1, parts + 1):
            pl.when((length + PART - 1) // PART == case)(functools.partial(act, case * PART))

    def start(cache, row):
        by_length(lengths[row], lambda count: copy(cache, row, count).start())

    def wait(cache, row):
        by_length(lengths[row], lambda count: copy(cache, row, count).wait())

    def clear(row, part):
        values[row, part * PART : (part + 1) * PART] = jnp.zeros(
            (PART, values.shape[2]), values.dtype
        )

    def score(row, wide, count):
        for group in range(KVH):
            heads = pl.ds(group * share, share)
            wide[heads, group * HD : (group + 1) * HD] = query[row, heads]
        scores = lax.dot_general(
            wide[...],
            keys[row, :count],
            (((1,), (1,)), ((), ())),
            preferred_element_type=jnp.float32,
        )
        position = lax.broadcasted_iota(jnp.int32, scores.shape, 1)
        return jnp.where(position < lengths[row], scores * scale, -jnp.inf)

    def weigh(row, scores):
        fresh_key = jnp.broadcast_to(key_new[row][:, None, :], (KVH, share, HD))
        fresh_key = fresh_key.reshape(HQ, HD).astype(jnp.float32)
        fresh = jnp.sum(query[row].astype(jnp.float32) * fresh_key, axis=1, keepdims=True) * scale
        top = jnp.maximum(jnp.max(scores, axis=1, keepdims=True), fresh)
        probs = jnp.exp(scores - top)
        pnew = jnp.exp(fresh - top)
        unit = 1.0 / (jnp.sum(probs, axis=1, keepdims=True) + pnew)
        weights = (probs * unit).astype(jnp.bfloat16)
        return weights, (pnew * unit).astype(jnp.bfloat16).astype(jnp.float32)

    def mix(row, weights, wnew, count):
        mixed = jnp.dot(weights, values[row, :count], preferred_element_type=jnp.float32)
        for group in range(KVH):
            heads = slice(group * share, (group + 1) * share)
            own = mixed[heads, group * HD : (group + 1) * HD]
            own = own + wnew[heads] * value_new[row, group : group + 1]
            out[row, heads] = own.astype(out.dtype)

    def group(row, count):
        each = [row + at for at in range(GROUP)]
        for one in each:
            wait(0, one)
            for part in range(1, count // PART):
                pl.when(lengths[one] <= part * PART)(functools.partial(clear, one, part))
        scores = [score(one, wide.at[at], count) for at, one in enumerate(each)]
        weighed = [weigh(one, of_one) for one, of_one in zip(each, scores)]
        for one in each:
            wait(1, one)
        for one, (weights, wnew) in zip(each, weighed):
            mix(one, weights, wnew, count)

    @pl.loop(0, rows // GROUP)
    def _(index):
        for cache in range(2):

            @pl.loop(0, GROUP)
            def _(at):
                start(cache, index * GROUP + at)

    wide[...] = jnp.zeros_like(wide)

    @pl.loop(0, rows // GROUP)
    def _(index):
        row = index * GROUP
        longest = lengths[row]
        for at in range(1, GROUP):
            longest = jnp.maximum(longest, lengths[row + at])
        by_length(longest, functools.partial(group, row))


def attend_local(owned, k_cache, v_cache, lengths):
    rows = owned.shape[0]
    query = owned[:, : HQ * HD].reshape(rows, HQ, HD).astype(jnp.float32)
    key_new = owned[:, HQ * HD : (HQ + KVH) * HD].reshape(rows, KVH, HD).astype(jnp.float32)
    value_new = owned[:, (HQ + KVH) * HD :].reshape(rows, KVH, HD).astype(jnp.float32)
    position = lengths.astype(jnp.float32)
    query = rotate(query, position, HD).astype(jnp.bfloat16)
    key_new = rotate(key_new, position, HD).astype(jnp.bfloat16)
    span, width = k_cache.shape[1:]
    vmem = pl.BlockSpec(memory_space=pltpu.VMEM)
    anywhere = pl.BlockSpec(memory_space=pl.ANY)
    mixed = pl.pallas_call(
        attend_kernel,
        in_specs=[
            pl.BlockSpec(memory_space=pltpu.SMEM),
            vmem,
            vmem,
            vmem,
            anywhere,
            anywhere,
        ],
        out_specs=vmem,
        out_shape=jax.ShapeDtypeStruct((rows, HQ, HD), jnp.bfloat16),
        scratch_shapes=[
            pltpu.VMEM((rows, span, width), jnp.bfloat16),
            pltpu.VMEM((rows, span, width), jnp.bfloat16),
            pltpu.VMEM((GROUP, HQ, width), jnp.bfloat16),
            pltpu.SemaphoreType.DMA((rows, 2)),
        ],
        compiler_params=pltpu.CompilerParams(vmem_limit_bytes=ROOM),
        cost_estimate=pl.CostEstimate(
            flops=4 * rows * span * width * HQ,
            bytes_accessed=2 * rows * span * width,
            transcendentals=rows * span * HQ,
        ),
    )(lengths, query, key_new, value_new, k_cache, v_cache)
    return mixed.reshape(rows, HQ * HD)


def swap(block, axis, bit):
    count = lax.axis_size(axis)
    return lax.ppermute(block, axis, [(i, i ^ bit) for i in range(count)])


def all_rows(block):
    if lax.axis_size("gx") != 8:
        pieces = lax.all_gather(block, "gx", axis=0)
        count, rows, width = pieces.shape
        return pieces.reshape(count, 2, rows // 2, width).transpose(1, 0, 2, 3)
    mine = [block] + [swap(block, "gx", chip) for chip in (2, 4, 6)]
    theirs = [swap(piece, "gx", 1) for piece in mine]
    pieces = [piece for pair in zip(mine, theirs) for piece in pair]
    halves = [piece.reshape(2, 1, -1, block.shape[1]) for piece in pieces]
    return jnp.concatenate(halves, axis=1)


def multiply_kernel(start, far, near, weights, out, held, sems):
    parts, depth, columns = held.shape

    def copy(part):
        return pltpu.make_async_copy(
            weights.at[pl.ds(part * depth, depth), pl.ds(start, columns)],
            held.at[part],
            sems.at[part],
        )

    for part in range(parts):
        copy(part).start()
    out[...] = jnp.zeros_like(out)

    @pl.loop(0, parts)
    def _(part):
        copy(part).wait()
        some = pl.ds(pl.multiple_of(part * depth, depth), depth)
        rows = jnp.concatenate([far[:, some], near[:, some]], axis=0)
        out[...] += jnp.dot(rows, held[part], preferred_element_type=jnp.float32)


def multiply(far, near, weights, start, columns):
    half, width = far.shape
    depth = 512
    vmem = pl.BlockSpec(memory_space=pltpu.VMEM)
    return pl.pallas_call(
        functools.partial(multiply_kernel, start),
        in_specs=[vmem, vmem, pl.BlockSpec(memory_space=pl.ANY)],
        out_specs=vmem,
        out_shape=jax.ShapeDtypeStruct((2 * half, columns), jnp.float32),
        scratch_shapes=[
            pltpu.VMEM((width // depth, depth, columns), jnp.bfloat16),
            pltpu.SemaphoreType.DMA((width // depth,)),
        ],
        compiler_params=pltpu.CompilerParams(vmem_limit_bytes=ROOM),
        cost_estimate=pl.CostEstimate(
            flops=4 * half * width * columns,
            bytes_accessed=2 * width * columns,
            transcendentals=0,
        ),
    )(far, near, weights)


def project(rows, weights, scale):
    width, columns = weights.shape
    here = lax.axis_index("gy")

    def features(owner):
        return lax.dynamic_slice_in_dim(rows, owner * width, width, axis=1)

    def pack(values):
        return (values * scale).astype(jnp.float16)

    def send(packed, bit):
        return swap(packed, "gy", bit).astype(jnp.float32) * (1.0 / scale)

    near, far, last = (swap(features(here ^ bit), "gy", bit) for bit in (1, 2, 3))
    near = jnp.concatenate([features(here), near])
    far = all_rows(jnp.concatenate([far, last]))
    near = all_rows(near)
    shape = (2, 2) + far.shape[1:3]
    far = far.reshape(-1, width)
    near = near.reshape(-1, width)
    first = columns // 512 * 256 if columns % 256 == 0 else columns
    left = multiply(far, near, weights, 0, first).reshape(shape + (first,))
    go_left = pack(left[:, 1])
    go_left, far, near = lax.optimization_barrier((go_left, far, near))
    left = left[:, 0] + send(go_left, 1)
    if first == columns:
        return [left[1] + send(pack(left[0]), 2)]
    right = multiply(far, near, weights, first, columns - first)
    right = right.reshape(shape + (columns - first,))
    go_far = pack(right[0, 1])
    across, go_near = lax.optimization_barrier((pack(left[0]), pack(right[1, 1])))
    left = left[1] + send(across, 2)
    across = pack(right[0, 0] + send(go_far, 1))
    right = right[1, 0] + send(go_near, 1) + send(across, 2)
    return [left, right]


def collect(columns):
    columns = columns.astype(jnp.bfloat16)
    count, rows, width = columns.shape
    if count != 8:
        return lax.all_to_all(columns, "gx", split_axis=0, concat_axis=0)
    pairs = [columns[:2]] + [
        swap(columns[chip : chip + 2], "gx", chip) for chip in (2, 4, 6)
    ]
    theirs = swap(jnp.stack([pair[1] for pair in pairs]), "gx", 1)
    owned = jnp.stack([pair[0] for pair in pairs])
    return jnp.stack([owned, theirs], axis=1).reshape(count, rows, width)


def deliver(parts):
    owned = jnp.concatenate([collect(part) for part in parts], axis=-1)
    count, rows, width = owned.shape
    if count == 8:
        owned = owned[jnp.arange(count) ^ lax.axis_index("gx")]
    return owned.transpose(1, 0, 2).reshape(rows, count * width)


def level(rows):
    rows = rows.astype(jnp.float32)
    top = jnp.max(jnp.abs(rows), axis=-1, keepdims=True)
    scale = jnp.ones_like(top)
    unit = jnp.ones_like(top)
    for power in (64, 32, 16, 8, 4, 2, 1):
        large = top * scale > 2.0 ** (power - 1)
        scale = jnp.where(large, scale * 2.0**-power, scale)
        unit = jnp.where(large, unit * 2.0**power, unit)
    for power in (64, 32, 16, 8, 4, 2, 1):
        small = top * scale <= 2.0**-power
        scale = jnp.where(small, scale * 2.0**power, scale)
        unit = jnp.where(small, unit * 2.0**-power, unit)
    return (rows * scale).astype(jnp.bfloat16), unit


def norm_kernel(hidden_hbm, gain_hbm, out, hidden, gain, sems):
    copies = (
        pltpu.make_async_copy(hidden_hbm, hidden, sems.at[0]),
        pltpu.make_async_copy(gain_hbm, gain, sems.at[1]),
    )
    for copy in copies:
        copy.start()
    for copy in copies:
        copy.wait()
    widened = hidden[...].astype(jnp.float32)
    mean = jnp.mean(widened * widened, axis=-1, keepdims=True)
    out[...] = (widened * lax.rsqrt(mean + eps) * gain[...]).astype(out.dtype)


def norm(hidden_in, norm_gain):
    anywhere = pl.BlockSpec(memory_space=pl.ANY)
    gain = norm_gain.reshape(1, -1)
    return pl.pallas_call(
        norm_kernel,
        in_specs=[anywhere, anywhere],
        out_specs=pl.BlockSpec(memory_space=pltpu.VMEM),
        out_shape=jax.ShapeDtypeStruct(hidden_in.shape, jnp.bfloat16),
        scratch_shapes=[
            pltpu.VMEM(hidden_in.shape, hidden_in.dtype),
            pltpu.VMEM(gain.shape, gain.dtype),
            pltpu.SemaphoreType.DMA((2,)),
        ],
        compiler_params=pltpu.CompilerParams(vmem_limit_bytes=62 * 2**20),
    )(hidden_in, gain)


def on_device(hidden_in, norm_gain, w_qkv, k_cache, v_cache, lengths, w_out):
    normed = norm(hidden_in, norm_gain)
    qkv = project(normed, w_qkv, 32.0)
    owned = deliver(qkv)
    attended = attend_local(owned, k_cache, v_cache, lengths)
    scaled, unit = level(attended)
    out = deliver([jnp.concatenate(project(scaled, w_out, 8.0), axis=-1)])
    return (out.astype(jnp.float32) * unit).astype(jnp.bfloat16)


def solution(mesh):
    return jax.shard_map(
        on_device,
        mesh=mesh,
        in_specs=(
            P(("gx", "gy"), None),
            P(),
            P("gy", "gx"),
            P(("gx", "gy"), None, None),
            P(("gx", "gy"), None, None),
            P(("gx", "gy")),
            P("gy", "gx"),
        ),
        out_specs=P(("gx", "gy"), None),
        check_vma=False,
    )
```

```python
import functools
import math

import jax
import jax.numpy as jnp
from jax import lax
from jax.experimental import pallas as pl
from jax.experimental.pallas import tpu as pltpu
from jax.sharding import PartitionSpec as P

HQ = 128
KVH = 8
HD = 128


eps = 1e-05
theta = 500000.0
ROOM = 50 * 2**20


def rotate(values, position, head_size):
    half = head_size // 2
    index = jnp.arange(half, dtype=jnp.float32)
    freqs = theta ** (-2.0 * index / head_size)
    angle = position[:, None, None] * freqs[None, None, :]
    cosine = jnp.cos(angle)
    sine = jnp.sin(angle)
    first = values[..., :half]
    second = values[..., half:]
    return jnp.concatenate(
        [first * cosine - second * sine, second * cosine + first * sine], axis=-1
    )


PART = 128
GROUP = 4
EARLY = 4
FETCH_ROOM = 38 * 2**20
ATTEND_ROOM = 44 * 2**20


def by_length(length, span, act):
    for case in range(1, span // PART + 1):
        pl.when((length + PART - 1) // PART == case)(functools.partial(act, case * PART))


def cache_copies(lengths, k_cache, v_cache, keys, values, sems, first):
    pairs = ((k_cache, keys), (v_cache, values))

    def copy(cache, at, count):
        source, target = pairs[cache]
        some = pl.ds(0, count)
        return pltpu.make_async_copy(
            source.at[first + at, some], target.at[at, some], sems.at[at, cache]
        )

    def start(cache, at):
        by_length(
            lengths[first + at], keys.shape[1], lambda count: copy(cache, at, count).start()
        )

    def wait(cache, at):
        by_length(
            lengths[first + at], keys.shape[1], lambda count: copy(cache, at, count).wait()
        )

    def clear(at):
        for part in range(1, values.shape[1] // PART):

            @pl.when(lengths[first + at] <= part * PART)
            def _():
                values[at, part * PART : (part + 1) * PART] = jnp.zeros(
                    (PART, values.shape[2]), values.dtype
                )

    return start, wait, clear


def fetch_kernel(lengths, k_cache, v_cache, keys, values, sems):
    rows = keys.shape[0]
    start, wait, clear = cache_copies(lengths, k_cache, v_cache, keys, values, sems, 0)
    for act in (start, wait):
        for cache in range(2):
            for at in range(rows):
                act(cache, at)
        if act is start:
            for at in range(rows):
                clear(at)


def fetch(lengths, k_cache, v_cache):
    vmem = pl.BlockSpec(memory_space=pltpu.VMEM)
    anywhere = pl.BlockSpec(memory_space=pl.ANY)
    shape = jax.ShapeDtypeStruct((EARLY,) + k_cache.shape[1:], k_cache.dtype)
    return pl.pallas_call(
        fetch_kernel,
        in_specs=[pl.BlockSpec(memory_space=pltpu.SMEM), anywhere, anywhere],
        out_specs=[vmem, vmem],
        out_shape=[shape, shape],
        scratch_shapes=[pltpu.SemaphoreType.DMA((EARLY, 2))],
        compiler_params=pltpu.CompilerParams(vmem_limit_bytes=FETCH_ROOM),
        cost_estimate=pl.CostEstimate(
            flops=0, bytes_accessed=4 * EARLY * shape.shape[1] * shape.shape[2], transcendentals=0
        ),
    )(lengths, k_cache, v_cache)


def attend_kernel(
    lengths, query, key_new, value_new, early_keys, early_values, k_cache, v_cache, out,
    keys, values, wide, sems,
):
    rows = query.shape[0]
    span = keys.shape[1]
    early = early_keys.shape[0]
    share = HQ // KVH
    scale = 1.0 / math.sqrt(HD)
    start, wait, clear = cache_copies(lengths, k_cache, v_cache, keys, values, sems, early)

    def score(row, row_keys, wide):
        for group in range(KVH):
            heads = pl.ds(group * share, share)
            wide[heads, group * HD : (group + 1) * HD] = query[row, heads]
        scores = lax.dot_general(
            wide[...],
            row_keys,
            (((1,), (1,)), ((), ())),
            preferred_element_type=jnp.float32,
        )
        position = lax.broadcasted_iota(jnp.int32, scores.shape, 1)
        return jnp.where(position < lengths[row], scores * scale, -jnp.inf)

    def weigh(row, scores):
        fresh_key = jnp.broadcast_to(key_new[row][:, None, :], (KVH, share, HD))
        fresh_key = fresh_key.reshape(HQ, HD).astype(jnp.float32)
        fresh = jnp.sum(query[row].astype(jnp.float32) * fresh_key, axis=1, keepdims=True) * scale
        top = jnp.maximum(jnp.max(scores, axis=1, keepdims=True), fresh)
        probs = jnp.exp(scores - top)
        pnew = jnp.exp(fresh - top)
        unit = 1.0 / (jnp.sum(probs, axis=1, keepdims=True) + pnew)
        weights = (probs * unit).astype(jnp.bfloat16)
        return weights, (pnew * unit).astype(jnp.bfloat16).astype(jnp.float32)

    def mix(row, weights, wnew, row_values):
        mixed = jnp.dot(weights, row_values, preferred_element_type=jnp.float32)
        for group in range(KVH):
            heads = slice(group * share, (group + 1) * share)
            own = mixed[heads, group * HD : (group + 1) * HD]
            own = own + wnew[heads] * value_new[row, group : group + 1]
            out[row, heads] = own.astype(out.dtype)

    def group(first, base, late, count):
        some_keys, some_values = (keys, values) if late else (early_keys, early_values)
        each = range(GROUP)
        if late:
            for at in each:
                wait(0, base + at)
        scores = [
            score(first + at, some_keys[base + at, :count], wide.at[at]) for at in each
        ]
        weighed = [weigh(first + at, scores[at]) for at in each]
        if late:
            for at in each:
                wait(1, base + at)
        for at, (weights, wnew) in zip(each, weighed):
            mix(first + at, weights, wnew, some_values[base + at, :count])

    for base in range(0, rows - early, GROUP):
        for cache in range(2):
            for at in range(GROUP):
                start(cache, base + at)
    wide[...] = jnp.zeros_like(wide)
    for at in range(rows - early):
        clear(at)
    for first in range(0, rows, GROUP):
        longest = lengths[first]
        for at in range(1, GROUP):
            longest = jnp.maximum(longest, lengths[first + at])
        late = first >= early
        base = first - early if late else first
        by_length(longest, span, functools.partial(group, first, base, late))


def attend_local(owned, early, k_cache, v_cache, lengths):
    rows = owned.shape[0]
    query = owned[:, : HQ * HD].reshape(rows, HQ, HD).astype(jnp.float32)
    key_new = owned[:, HQ * HD : (HQ + KVH) * HD].reshape(rows, KVH, HD).astype(jnp.float32)
    value_new = owned[:, (HQ + KVH) * HD :].reshape(rows, KVH, HD).astype(jnp.float32)
    position = lengths.astype(jnp.float32)
    query = rotate(query, position, HD).astype(jnp.bfloat16)
    key_new = rotate(key_new, position, HD).astype(jnp.bfloat16)
    span, width = k_cache.shape[1:]
    vmem = pl.BlockSpec(memory_space=pltpu.VMEM)
    anywhere = pl.BlockSpec(memory_space=pl.ANY)
    mixed = pl.pallas_call(
        attend_kernel,
        in_specs=[pl.BlockSpec(memory_space=pltpu.SMEM)] + [vmem] * 5 + [anywhere] * 2,
        out_specs=vmem,
        out_shape=jax.ShapeDtypeStruct((rows, HQ, HD), jnp.bfloat16),
        scratch_shapes=[
            pltpu.VMEM((rows - EARLY, span, width), jnp.bfloat16),
            pltpu.VMEM((rows - EARLY, span, width), jnp.bfloat16),
            pltpu.VMEM((GROUP, HQ, width), jnp.bfloat16),
            pltpu.SemaphoreType.DMA((rows - EARLY, 2)),
        ],
        compiler_params=pltpu.CompilerParams(vmem_limit_bytes=ATTEND_ROOM),
        cost_estimate=pl.CostEstimate(
            flops=4 * rows * span * width * HQ,
            bytes_accessed=2 * rows * span * width,
            transcendentals=rows * span * HQ,
        ),
    )(lengths, query, key_new, value_new, *early, k_cache, v_cache)
    return mixed.reshape(rows, HQ * HD)


def swap(block, axis, bit):
    count = lax.axis_size(axis)
    return lax.ppermute(block, axis, [(i, i ^ bit) for i in range(count)])


def all_rows(block):
    if lax.axis_size("gx") != 8:
        pieces = lax.all_gather(block, "gx", axis=0)
        count, rows, width = pieces.shape
        return pieces.reshape(count, 2, rows // 2, width).transpose(1, 0, 2, 3)
    other = swap(block, "gx", 1)
    later = lax.optimization_barrier((block, other))[0]
    mine = [swap(block, "gx", 2), swap(block, "gx", 4), swap(later, "gx", 6)]
    theirs = [other] + [swap(piece, "gx", 1) for piece in mine]
    mine = [block] + mine
    pieces = [piece for pair in zip(mine, theirs) for piece in pair]
    halves = [piece.reshape(2, 1, -1, block.shape[1]) for piece in pieces]
    return jnp.concatenate(halves, axis=1)


def multiply_kernel(start, far, near, weights, out, held, sems):
    parts, depth, columns = held.shape

    def copy(part):
        return pltpu.make_async_copy(
            weights.at[pl.ds(part * depth, depth), pl.ds(start, columns)],
            held.at[part],
            sems.at[part],
        )

    for part in range(parts):
        copy(part).start()
    out[...] = jnp.zeros_like(out)

    @pl.loop(0, parts)
    def _(part):
        copy(part).wait()
        some = pl.ds(pl.multiple_of(part * depth, depth), depth)
        rows = jnp.concatenate([far[:, some], near[:, some]], axis=0)
        out[...] += jnp.dot(rows, held[part], preferred_element_type=jnp.float32)


def multiply(far, near, weights, start, columns):
    half, width = far.shape
    depth = 512
    vmem = pl.BlockSpec(memory_space=pltpu.VMEM)
    return pl.pallas_call(
        functools.partial(multiply_kernel, start),
        in_specs=[vmem, vmem, pl.BlockSpec(memory_space=pl.ANY)],
        out_specs=vmem,
        out_shape=jax.ShapeDtypeStruct((2 * half, columns), jnp.float32),
        scratch_shapes=[
            pltpu.VMEM((width // depth, depth, columns), jnp.bfloat16),
            pltpu.SemaphoreType.DMA((width // depth,)),
        ],
        compiler_params=pltpu.CompilerParams(vmem_limit_bytes=ROOM),
        cost_estimate=pl.CostEstimate(
            flops=4 * half * width * columns,
            bytes_accessed=2 * width * columns,
            transcendentals=0,
        ),
    )(far, near, weights)


def project(rows, weights, scale, beside=None):
    width, columns = weights.shape
    here = lax.axis_index("gy")

    def features(owner):
        return lax.dynamic_slice_in_dim(rows, owner * width, width, axis=1)

    def pack(values):
        return (values * scale).astype(jnp.float16)

    def send(packed, bit):
        return swap(packed, "gy", bit).astype(jnp.float32) * (1.0 / scale)

    near, far, last = (swap(features(here ^ bit), "gy", bit) for bit in (1, 2, 3))
    near = jnp.concatenate([features(here), near])
    far = all_rows(jnp.concatenate([far, last]))
    near = all_rows(near)
    shape = (2, 2) + far.shape[1:3]
    far = far.reshape(-1, width)
    near = near.reshape(-1, width)
    first = columns // 512 * 256 if columns % 256 == 0 else columns
    left = multiply(far, near, weights, 0, first).reshape(shape + (first,))
    go_left = pack(left[:, 1])
    go_left, far, near = lax.optimization_barrier((go_left, far, near))
    left = left[:, 0] + send(go_left, 1)
    if first == columns:
        return [left[1] + send(pack(left[0]), 2)], beside and beside(go_left)
    right = multiply(far, near, weights, first, columns - first)
    right = right.reshape(shape + (columns - first,))
    go_far = pack(right[0, 1])
    across, go_near = lax.optimization_barrier((pack(left[0]), pack(right[1, 1])))
    others = beside and beside(across)
    left = left[1] + send(across, 2)
    across = pack(right[0, 0] + send(go_far, 1))
    right = right[1, 0] + send(go_near, 1) + send(across, 2)
    return [left, right], others


def collect(columns):
    columns = columns.astype(jnp.bfloat16)
    count, rows, width = columns.shape
    if count != 8:
        return lax.all_to_all(columns, "gx", split_axis=0, concat_axis=0)
    pairs = [columns[:2]] + [
        swap(columns[chip : chip + 2], "gx", chip) for chip in (2, 4, 6)
    ]
    theirs = swap(jnp.stack([pair[1] for pair in pairs]), "gx", 1)
    owned = jnp.stack([pair[0] for pair in pairs])
    return jnp.stack([owned, theirs], axis=1).reshape(count, rows, width)


def deliver(parts):
    owned = jnp.concatenate([collect(part) for part in parts], axis=-1)
    count, rows, width = owned.shape
    if count == 8:
        owned = owned[jnp.arange(count) ^ lax.axis_index("gx")]
    return owned.transpose(1, 0, 2).reshape(rows, count * width)


def level(rows):
    rows = rows.astype(jnp.float32)
    top = jnp.max(jnp.abs(rows), axis=-1, keepdims=True)
    scale = jnp.ones_like(top)
    unit = jnp.ones_like(top)
    for power in (64, 32, 16, 8, 4, 2, 1):
        large = top * scale > 2.0 ** (power - 1)
        scale = jnp.where(large, scale * 2.0**-power, scale)
        unit = jnp.where(large, unit * 2.0**power, unit)
    for power in (64, 32, 16, 8, 4, 2, 1):
        small = top * scale <= 2.0**-power
        scale = jnp.where(small, scale * 2.0**power, scale)
        unit = jnp.where(small, unit * 2.0**-power, unit)
    return (rows * scale).astype(jnp.bfloat16), unit


def on_device(hidden_in, norm_gain, w_qkv, k_cache, v_cache, lengths, w_out):
    widened = hidden_in.astype(jnp.float32)
    normed = (
        widened * lax.rsqrt(jnp.mean(widened * widened, axis=-1, keepdims=True) + eps) * norm_gain
    ).astype(jnp.bfloat16)
    def caches(ready):
        return fetch(lax.optimization_barrier((lengths, ready))[0], k_cache, v_cache)

    qkv, early = project(normed, w_qkv, 32.0, caches)
    attended = attend_local(deliver(qkv), early, k_cache, v_cache, lengths)
    scaled, unit = level(attended)
    out, _ = project(scaled, w_out, 8.0)
    out = deliver([jnp.concatenate(out, axis=-1)])
    return (out.astype(jnp.float32) * unit).astype(jnp.bfloat16)


def solution(mesh):
    return jax.shard_map(
        on_device,
        mesh=mesh,
        in_specs=(
            P(("gx", "gy"), None),
            P(),
            P("gy", "gx"),
            P(("gx", "gy"), None, None),
            P(("gx", "gy"), None, None),
            P(("gx", "gy")),
            P("gy", "gx"),
        ),
        out_specs=P(("gx", "gy"), None),
        check_vma=False,
    )
```

```python
import functools
import math

import jax
import jax.numpy as jnp
from jax import lax
from jax.experimental import pallas as pl
from jax.experimental.pallas import tpu as pltpu
from jax.sharding import PartitionSpec as P

HQ = 128
KVH = 8
HD = 128


eps = 1e-05
theta = 500000.0
ROOM = 50 * 2**20


def rotate(values, position, head_size):
    half = head_size // 2
    index = jnp.arange(half, dtype=jnp.float32)
    freqs = theta ** (-2.0 * index / head_size)
    angle = position[:, None, None] * freqs[None, None, :]
    cosine = jnp.cos(angle)
    sine = jnp.sin(angle)
    first = values[..., :half]
    second = values[..., half:]
    return jnp.concatenate(
        [first * cosine - second * sine, second * cosine + first * sine], axis=-1
    )


PART = 128
GROUP = 4


def attend_kernel(lengths, query, key_new, value_new, k_cache, v_cache, out, keys, values, wide, sems):
    rows, span = keys.shape[:2]
    share = HQ // KVH
    parts = span // PART
    scale = 1.0 / math.sqrt(HD)

    def copy(cache, row, count):
        source, target = ((k_cache, keys), (v_cache, values))[cache]
        some = pl.ds(0, count)
        return pltpu.make_async_copy(
            source.at[row, some], target.at[row, some], sems.at[row, cache]
        )

    def by_length(length, act):
        for case in range(1, parts + 1):
            pl.when((length + PART - 1) // PART == case)(functools.partial(act, case * PART))

    def start(cache, row):
        by_length(lengths[row], lambda count: copy(cache, row, count).start())

    def wait(cache, row):
        by_length(lengths[row], lambda count: copy(cache, row, count).wait())

    def clear(row, part):
        values[row, part * PART : (part + 1) * PART] = jnp.zeros(
            (PART, values.shape[2]), values.dtype
        )

    def score(row, wide, count):
        for group in range(KVH):
            heads = pl.ds(group * share, share)
            side = group % 2 * HD
            wide[heads, side : side + HD] = query[row, heads]
        scores = [
            lax.dot_general(
                wide[2 * share * pair : 2 * share * (pair + 1)],
                keys[row, :count, 2 * HD * pair : 2 * HD * (pair + 1)],
                (((1,), (1,)), ((), ())),
                preferred_element_type=jnp.float32,
            )
            for pair in range(KVH // 2)
        ]
        scores = jnp.concatenate(scores, axis=0)
        position = lax.broadcasted_iota(jnp.int32, scores.shape, 1)
        return jnp.where(position < lengths[row], scores * scale, -jnp.inf)

    def weigh(row, scores):
        fresh_key = jnp.broadcast_to(key_new[row][:, None, :], (KVH, share, HD))
        fresh_key = fresh_key.reshape(HQ, HD).astype(jnp.float32)
        fresh = jnp.sum(query[row].astype(jnp.float32) * fresh_key, axis=1, keepdims=True) * scale
        top = jnp.maximum(jnp.max(scores, axis=1, keepdims=True), fresh)
        probs = jnp.exp(scores - top)
        pnew = jnp.exp(fresh - top)
        unit = 1.0 / (jnp.sum(probs, axis=1, keepdims=True) + pnew)
        weights = (probs * unit).astype(jnp.bfloat16)
        return weights, (pnew * unit).astype(jnp.bfloat16).astype(jnp.float32)

    def mix(row, weights, wnew, count):
        for pair in range(KVH // 2):
            mixed = jnp.dot(
                weights[2 * share * pair : 2 * share * (pair + 1)],
                values[row, :count, 2 * HD * pair : 2 * HD * (pair + 1)],
                preferred_element_type=jnp.float32,
            )
            for side in range(2):
                group = 2 * pair + side
                heads = slice(group * share, (group + 1) * share)
                own = mixed[side * share : (side + 1) * share, side * HD : (side + 1) * HD]
                own = own + wnew[heads] * value_new[row, group : group + 1]
                out[row, heads] = own.astype(out.dtype)

    def group(row, count):
        each = [row + at for at in range(GROUP)]
        for one in each:
            wait(0, one)
            for part in range(1, count // PART):
                pl.when(lengths[one] <= part * PART)(functools.partial(clear, one, part))
        scores = [score(one, wide.at[at], count) for at, one in enumerate(each)]
        weighed = [weigh(one, of_one) for one, of_one in zip(each, scores)]
        for one in each:
            wait(1, one)
        for one, (weights, wnew) in zip(each, weighed):
            mix(one, weights, wnew, count)

    @pl.loop(0, rows // GROUP)
    def _(index):
        for cache in range(2):

            @pl.loop(0, GROUP)
            def _(at):
                start(cache, index * GROUP + at)

    wide[...] = jnp.zeros_like(wide)

    @pl.loop(0, rows // GROUP)
    def _(index):
        row = index * GROUP
        longest = lengths[row]
        for at in range(1, GROUP):
            longest = jnp.maximum(longest, lengths[row + at])
        by_length(longest, functools.partial(group, row))


def attend_local(owned, k_cache, v_cache, lengths):
    rows = owned.shape[0]
    query = owned[:, : HQ * HD].reshape(rows, HQ, HD).astype(jnp.float32)
    key_new = owned[:, HQ * HD : (HQ + KVH) * HD].reshape(rows, KVH, HD).astype(jnp.float32)
    value_new = owned[:, (HQ + KVH) * HD :].reshape(rows, KVH, HD).astype(jnp.float32)
    position = lengths.astype(jnp.float32)
    query = rotate(query, position, HD).astype(jnp.bfloat16)
    key_new = rotate(key_new, position, HD).astype(jnp.bfloat16)
    span, width = k_cache.shape[1:]
    vmem = pl.BlockSpec(memory_space=pltpu.VMEM)
    anywhere = pl.BlockSpec(memory_space=pl.ANY)
    mixed = pl.pallas_call(
        attend_kernel,
        in_specs=[
            pl.BlockSpec(memory_space=pltpu.SMEM),
            vmem,
            vmem,
            vmem,
            anywhere,
            anywhere,
        ],
        out_specs=vmem,
        out_shape=jax.ShapeDtypeStruct((rows, HQ, HD), jnp.bfloat16),
        scratch_shapes=[
            pltpu.VMEM((rows, span, width), jnp.bfloat16),
            pltpu.VMEM((rows, span, width), jnp.bfloat16),
            pltpu.VMEM((GROUP, HQ, 2 * HD), jnp.bfloat16),
            pltpu.SemaphoreType.DMA((rows, 2)),
        ],
        compiler_params=pltpu.CompilerParams(vmem_limit_bytes=ROOM),
        cost_estimate=pl.CostEstimate(
            flops=4 * rows * span * width * HQ,
            bytes_accessed=2 * rows * span * width,
            transcendentals=rows * span * HQ,
        ),
    )(lengths, query, key_new, value_new, k_cache, v_cache)
    return mixed.reshape(rows, HQ * HD)


def swap(block, axis, bit):
    count = lax.axis_size(axis)
    return lax.ppermute(block, axis, [(i, i ^ bit) for i in range(count)])


def all_rows(block):
    if lax.axis_size("gx") != 8:
        pieces = lax.all_gather(block, "gx", axis=0)
        count, rows, width = pieces.shape
        return pieces.reshape(count, 2, rows // 2, width).transpose(1, 0, 2, 3)
    mine = [block] + [swap(block, "gx", chip) for chip in (2, 4, 6)]
    theirs = [swap(piece, "gx", 1) for piece in mine]
    pieces = [piece for pair in zip(mine, theirs) for piece in pair]
    halves = [piece.reshape(2, 1, -1, block.shape[1]) for piece in pieces]
    return jnp.concatenate(halves, axis=1)


def multiply_kernel(start, far, near, weights, out, held, sems):
    parts, depth, columns = held.shape

    def copy(part):
        return pltpu.make_async_copy(
            weights.at[pl.ds(part * depth, depth), pl.ds(start, columns)],
            held.at[part],
            sems.at[part],
        )

    for part in range(parts):
        copy(part).start()
    out[...] = jnp.zeros_like(out)

    @pl.loop(0, parts)
    def _(part):
        copy(part).wait()
        some = pl.ds(pl.multiple_of(part * depth, depth), depth)
        rows = jnp.concatenate([far[:, some], near[:, some]], axis=0)
        out[...] += jnp.dot(rows, held[part], preferred_element_type=jnp.float32)


def multiply(far, near, weights, start, columns):
    half, width = far.shape
    depth = 512
    vmem = pl.BlockSpec(memory_space=pltpu.VMEM)
    return pl.pallas_call(
        functools.partial(multiply_kernel, start),
        in_specs=[vmem, vmem, pl.BlockSpec(memory_space=pl.ANY)],
        out_specs=vmem,
        out_shape=jax.ShapeDtypeStruct((2 * half, columns), jnp.float32),
        scratch_shapes=[
            pltpu.VMEM((width // depth, depth, columns), jnp.bfloat16),
            pltpu.SemaphoreType.DMA((width // depth,)),
        ],
        compiler_params=pltpu.CompilerParams(vmem_limit_bytes=ROOM),
        cost_estimate=pl.CostEstimate(
            flops=4 * half * width * columns,
            bytes_accessed=2 * width * columns,
            transcendentals=0,
        ),
    )(far, near, weights)


def project(rows, weights, scale):
    width, columns = weights.shape
    here = lax.axis_index("gy")

    def features(owner):
        return lax.dynamic_slice_in_dim(rows, owner * width, width, axis=1)

    def pack(values):
        return (values * scale).astype(jnp.float16)

    def send(packed, bit):
        return swap(packed, "gy", bit).astype(jnp.float32) * (1.0 / scale)

    near, far, last = (swap(features(here ^ bit), "gy", bit) for bit in (1, 2, 3))
    near = jnp.concatenate([features(here), near])
    far = all_rows(jnp.concatenate([far, last]))
    near = all_rows(near)
    shape = (2, 2) + far.shape[1:3]
    far = far.reshape(-1, width)
    near = near.reshape(-1, width)
    first = columns // 512 * 256 if columns % 256 == 0 else columns
    left = multiply(far, near, weights, 0, first).reshape(shape + (first,))
    go_left = pack(left[:, 1])
    go_left, far, near = lax.optimization_barrier((go_left, far, near))
    left = left[:, 0] + send(go_left, 1)
    if first == columns:
        return [left[1] + send(pack(left[0]), 2)]
    right = multiply(far, near, weights, first, columns - first)
    right = right.reshape(shape + (columns - first,))
    go_far = pack(right[0, 1])
    across, go_near = lax.optimization_barrier((pack(left[0]), pack(right[1, 1])))
    left = left[1] + send(across, 2)
    across = pack(right[0, 0] + send(go_far, 1))
    right = right[1, 0] + send(go_near, 1) + send(across, 2)
    return [left, right]


def collect(columns):
    columns = columns.astype(jnp.bfloat16)
    count, rows, width = columns.shape
    if count != 8:
        return lax.all_to_all(columns, "gx", split_axis=0, concat_axis=0)
    pairs = [columns[:2]] + [
        swap(columns[chip : chip + 2], "gx", chip) for chip in (2, 4, 6)
    ]
    theirs = swap(jnp.stack([pair[1] for pair in pairs]), "gx", 1)
    owned = jnp.stack([pair[0] for pair in pairs])
    return jnp.stack([owned, theirs], axis=1).reshape(count, rows, width)


def deliver(parts):
    owned = jnp.concatenate([collect(part) for part in parts], axis=-1)
    count, rows, width = owned.shape
    if count == 8:
        owned = owned[jnp.arange(count) ^ lax.axis_index("gx")]
    return owned.transpose(1, 0, 2).reshape(rows, count * width)


def level(rows):
    rows = rows.astype(jnp.float32)
    top = jnp.max(jnp.abs(rows), axis=-1, keepdims=True)
    scale = jnp.ones_like(top)
    unit = jnp.ones_like(top)
    for power in (64, 32, 16, 8, 4, 2, 1):
        large = top * scale > 2.0 ** (power - 1)
        scale = jnp.where(large, scale * 2.0**-power, scale)
        unit = jnp.where(large, unit * 2.0**power, unit)
    for power in (64, 32, 16, 8, 4, 2, 1):
        small = top * scale <= 2.0**-power
        scale = jnp.where(small, scale * 2.0**power, scale)
        unit = jnp.where(small, unit * 2.0**-power, unit)
    return (rows * scale).astype(jnp.bfloat16), unit


def on_device(hidden_in, norm_gain, w_qkv, k_cache, v_cache, lengths, w_out):
    widened = hidden_in.astype(jnp.float32)
    normed = (
        widened * lax.rsqrt(jnp.mean(widened * widened, axis=-1, keepdims=True) + eps) * norm_gain
    ).astype(jnp.bfloat16)
    qkv = project(normed, w_qkv, 32.0)
    owned = deliver(qkv)
    attended = attend_local(owned, k_cache, v_cache, lengths)
    scaled, unit = level(attended)
    out = deliver([jnp.concatenate(project(scaled, w_out, 8.0), axis=-1)])
    return (out.astype(jnp.float32) * unit).astype(jnp.bfloat16)


def solution(mesh):
    return jax.shard_map(
        on_device,
        mesh=mesh,
        in_specs=(
            P(("gx", "gy"), None),
            P(),
            P("gy", "gx"),
            P(("gx", "gy"), None, None),
            P(("gx", "gy"), None, None),
            P(("gx", "gy")),
            P("gy", "gx"),
        ),
        out_specs=P(("gx", "gy"), None),
        check_vma=False,
    )
```

```python
import functools
import math

import jax
import jax.numpy as jnp
from jax import lax
from jax.experimental import pallas as pl
from jax.experimental.pallas import tpu as pltpu
from jax.sharding import PartitionSpec as P

HQ = 128
KVH = 8
HD = 128


eps = 1e-05
theta = 500000.0
ROOM = 50 * 2**20


def rotate(values, position, head_size):
    half = head_size // 2
    index = jnp.arange(half, dtype=jnp.float32)
    freqs = theta ** (-2.0 * index / head_size)
    angle = position[:, None, None] * freqs[None, None, :]
    cosine = jnp.cos(angle)
    sine = jnp.sin(angle)
    first = values[..., :half]
    second = values[..., half:]
    return jnp.concatenate(
        [first * cosine - second * sine, second * cosine + first * sine], axis=-1
    )


PART = 128
GROUP = 2


def attend_kernel(lengths, query, key_new, value_new, k_cache, v_cache, out, keys, values, wide, sems):
    rows, span = keys.shape[:2]
    share = HQ // KVH
    parts = span // PART
    scale = 1.0 / math.sqrt(HD)

    def copy(cache, row, count):
        source, target = ((k_cache, keys), (v_cache, values))[cache]
        some = pl.ds(0, count)
        return pltpu.make_async_copy(
            source.at[row, some], target.at[row, some], sems.at[row, cache]
        )

    def by_length(length, act):
        for case in range(1, parts + 1):
            pl.when((length + PART - 1) // PART == case)(functools.partial(act, case * PART))

    def start(cache, row):
        by_length(lengths[row], lambda count: copy(cache, row, count).start())

    def wait(cache, row):
        by_length(lengths[row], lambda count: copy(cache, row, count).wait())

    def clear(row, part):
        values[row, part * PART : (part + 1) * PART] = jnp.zeros(
            (PART, values.shape[2]), values.dtype
        )

    def score(row, wide, count):
        for group in range(KVH):
            heads = pl.ds(group * share, share)
            side = group % 2 * HD
            wide[heads, side : side + HD] = query[row, heads]
        scores = [
            lax.dot_general(
                wide[2 * share * pair : 2 * share * (pair + 1)],
                keys[row, :count, 2 * HD * pair : 2 * HD * (pair + 1)],
                (((1,), (1,)), ((), ())),
                preferred_element_type=jnp.float32,
            )
            for pair in range(KVH // 2)
        ]
        scores = jnp.concatenate(scores, axis=0)
        position = lax.broadcasted_iota(jnp.int32, scores.shape, 1)
        return jnp.where(position < lengths[row], scores * scale, -jnp.inf)

    def weigh(row, scores):
        fresh_key = jnp.broadcast_to(key_new[row][:, None, :], (KVH, share, HD))
        fresh_key = fresh_key.reshape(HQ, HD).astype(jnp.float32)
        fresh = jnp.sum(query[row].astype(jnp.float32) * fresh_key, axis=1, keepdims=True) * scale
        top = jnp.maximum(jnp.max(scores, axis=1, keepdims=True), fresh)
        probs = jnp.exp(scores - top)
        pnew = jnp.exp(fresh - top)
        unit = 1.0 / (jnp.sum(probs, axis=1, keepdims=True) + pnew)
        weights = (probs * unit).astype(jnp.bfloat16)
        return weights, (pnew * unit).astype(jnp.bfloat16).astype(jnp.float32)

    def mix(row, weights, wnew, count):
        for pair in range(KVH // 2):
            mixed = jnp.dot(
                weights[2 * share * pair : 2 * share * (pair + 1)],
                values[row, :count, 2 * HD * pair : 2 * HD * (pair + 1)],
                preferred_element_type=jnp.float32,
            )
            for side in range(2):
                group = 2 * pair + side
                heads = slice(group * share, (group + 1) * share)
                own = mixed[side * share : (side + 1) * share, side * HD : (side + 1) * HD]
                own = own + wnew[heads] * value_new[row, group : group + 1]
                out[row, heads] = own.astype(out.dtype)

    def group(row, count):
        each = [row + at for at in range(GROUP)]
        for one in each:
            wait(0, one)
            for part in range(1, count // PART):
                pl.when(lengths[one] <= part * PART)(functools.partial(clear, one, part))
        scores = [score(one, wide.at[at], count) for at, one in enumerate(each)]
        weighed = [weigh(one, of_one) for one, of_one in zip(each, scores)]
        for one in each:
            wait(1, one)
        for one, (weights, wnew) in zip(each, weighed):
            mix(one, weights, wnew, count)

    @pl.loop(0, rows // GROUP)
    def _(index):
        for cache in range(2):

            @pl.loop(0, GROUP)
            def _(at):
                start(cache, index * GROUP + at)

    wide[...] = jnp.zeros_like(wide)

    @pl.loop(0, rows // GROUP)
    def _(index):
        row = index * GROUP
        longest = lengths[row]
        for at in range(1, GROUP):
            longest = jnp.maximum(longest, lengths[row + at])
        by_length(longest, functools.partial(group, row))


def attend_local(owned, k_cache, v_cache, lengths):
    rows = owned.shape[0]
    query = owned[:, : HQ * HD].reshape(rows, HQ, HD).astype(jnp.float32)
    key_new = owned[:, HQ * HD : (HQ + KVH) * HD].reshape(rows, KVH, HD).astype(jnp.float32)
    value_new = owned[:, (HQ + KVH) * HD :].reshape(rows, KVH, HD).astype(jnp.float32)
    position = lengths.astype(jnp.float32)
    query = rotate(query, position, HD).astype(jnp.bfloat16)
    key_new = rotate(key_new, position, HD).astype(jnp.bfloat16)
    span, width = k_cache.shape[1:]
    vmem = pl.BlockSpec(memory_space=pltpu.VMEM)
    anywhere = pl.BlockSpec(memory_space=pl.ANY)
    mixed = pl.pallas_call(
        attend_kernel,
        in_specs=[
            pl.BlockSpec(memory_space=pltpu.SMEM),
            vmem,
            vmem,
            vmem,
            anywhere,
            anywhere,
        ],
        out_specs=vmem,
        out_shape=jax.ShapeDtypeStruct((rows, HQ, HD), jnp.bfloat16),
        scratch_shapes=[
            pltpu.VMEM((rows, span, width), jnp.bfloat16),
            pltpu.VMEM((rows, span, width), jnp.bfloat16),
            pltpu.VMEM((GROUP, HQ, 2 * HD), jnp.bfloat16),
            pltpu.SemaphoreType.DMA((rows, 2)),
        ],
        compiler_params=pltpu.CompilerParams(vmem_limit_bytes=ROOM),
        cost_estimate=pl.CostEstimate(
            flops=4 * rows * span * width * HQ,
            bytes_accessed=2 * rows * span * width,
            transcendentals=rows * span * HQ,
        ),
    )(lengths, query, key_new, value_new, k_cache, v_cache)
    return mixed.reshape(rows, HQ * HD)


def swap(block, axis, bit):
    count = lax.axis_size(axis)
    return lax.ppermute(block, axis, [(i, i ^ bit) for i in range(count)])


def all_rows(block):
    if lax.axis_size("gx") != 8:
        pieces = lax.all_gather(block, "gx", axis=0)
        count, rows, width = pieces.shape
        return pieces.reshape(count, 2, rows // 2, width).transpose(1, 0, 2, 3)
    mine = [block] + [swap(block, "gx", chip) for chip in (2, 4, 6)]
    theirs = [swap(piece, "gx", 1) for piece in mine]
    pieces = [piece for pair in zip(mine, theirs) for piece in pair]
    halves = [piece.reshape(2, 1, -1, block.shape[1]) for piece in pieces]
    return jnp.concatenate(halves, axis=1)


def multiply_kernel(start, far, near, weights, out, held, sems):
    parts, depth, columns = held.shape

    def copy(part):
        return pltpu.make_async_copy(
            weights.at[pl.ds(part * depth, depth), pl.ds(start, columns)],
            held.at[part],
            sems.at[part],
        )

    for part in range(parts):
        copy(part).start()
    out[...] = jnp.zeros_like(out)

    @pl.loop(0, parts)
    def _(part):
        copy(part).wait()
        some = pl.ds(pl.multiple_of(part * depth, depth), depth)
        rows = jnp.concatenate([far[:, some], near[:, some]], axis=0)
        out[...] += jnp.dot(rows, held[part], preferred_element_type=jnp.float32)


def multiply(far, near, weights, start, columns):
    half, width = far.shape
    depth = 512
    vmem = pl.BlockSpec(memory_space=pltpu.VMEM)
    return pl.pallas_call(
        functools.partial(multiply_kernel, start),
        in_specs=[vmem, vmem, pl.BlockSpec(memory_space=pl.ANY)],
        out_specs=vmem,
        out_shape=jax.ShapeDtypeStruct((2 * half, columns), jnp.float32),
        scratch_shapes=[
            pltpu.VMEM((width // depth, depth, columns), jnp.bfloat16),
            pltpu.SemaphoreType.DMA((width // depth,)),
        ],
        compiler_params=pltpu.CompilerParams(vmem_limit_bytes=ROOM),
        cost_estimate=pl.CostEstimate(
            flops=4 * half * width * columns,
            bytes_accessed=2 * width * columns,
            transcendentals=0,
        ),
    )(far, near, weights)


def project(rows, weights, scale):
    width, columns = weights.shape
    here = lax.axis_index("gy")

    def features(owner):
        return lax.dynamic_slice_in_dim(rows, owner * width, width, axis=1)

    def pack(values):
        return (values * scale).astype(jnp.float16)

    def send(packed, bit):
        return swap(packed, "gy", bit).astype(jnp.float32) * (1.0 / scale)

    near, far, last = (swap(features(here ^ bit), "gy", bit) for bit in (1, 2, 3))
    near = jnp.concatenate([features(here), near])
    far = all_rows(jnp.concatenate([far, last]))
    near = all_rows(near)
    shape = (2, 2) + far.shape[1:3]
    far = far.reshape(-1, width)
    near = near.reshape(-1, width)
    first = columns // 512 * 256 if columns % 256 == 0 else columns
    left = multiply(far, near, weights, 0, first).reshape(shape + (first,))
    go_left = pack(left[:, 1])
    go_left, far, near = lax.optimization_barrier((go_left, far, near))
    left = left[:, 0] + send(go_left, 1)
    if first == columns:
        return [left[1] + send(pack(left[0]), 2)]
    right = multiply(far, near, weights, first, columns - first)
    right = right.reshape(shape + (columns - first,))
    go_far = pack(right[0, 1])
    across, go_near = lax.optimization_barrier((pack(left[0]), pack(right[1, 1])))
    left = left[1] + send(across, 2)
    across = pack(right[0, 0] + send(go_far, 1))
    right = right[1, 0] + send(go_near, 1) + send(across, 2)
    return [left, right]


def collect(columns):
    columns = columns.astype(jnp.bfloat16)
    count, rows, width = columns.shape
    if count != 8:
        return lax.all_to_all(columns, "gx", split_axis=0, concat_axis=0)
    pairs = [columns[:2]] + [
        swap(columns[chip : chip + 2], "gx", chip) for chip in (2, 4, 6)
    ]
    theirs = swap(jnp.stack([pair[1] for pair in pairs]), "gx", 1)
    owned = jnp.stack([pair[0] for pair in pairs])
    return jnp.stack([owned, theirs], axis=1).reshape(count, rows, width)


def deliver(parts):
    owned = jnp.concatenate([collect(part) for part in parts], axis=-1)
    count, rows, width = owned.shape
    if count != 8:
        return owned.transpose(1, 0, 2).reshape(rows, count * width)
    me = lax.axis_index("gx")
    blocks = [lax.dynamic_index_in_dim(owned, at ^ me, keepdims=False) for at in range(count)]
    return jnp.concatenate(blocks, axis=1)


def level(rows):
    rows = rows.astype(jnp.float32)
    top = jnp.max(jnp.abs(rows), axis=-1, keepdims=True)
    scale = jnp.ones_like(top)
    unit = jnp.ones_like(top)
    for power in (64, 32, 16, 8, 4, 2, 1):
        large = top * scale > 2.0 ** (power - 1)
        scale = jnp.where(large, scale * 2.0**-power, scale)
        unit = jnp.where(large, unit * 2.0**power, unit)
    for power in (64, 32, 16, 8, 4, 2, 1):
        small = top * scale <= 2.0**-power
        scale = jnp.where(small, scale * 2.0**power, scale)
        unit = jnp.where(small, unit * 2.0**-power, unit)
    return (rows * scale).astype(jnp.bfloat16), unit


def on_device(hidden_in, norm_gain, w_qkv, k_cache, v_cache, lengths, w_out):
    widened = hidden_in.astype(jnp.float32)
    normed = (
        widened * lax.rsqrt(jnp.mean(widened * widened, axis=-1, keepdims=True) + eps) * norm_gain
    ).astype(jnp.bfloat16)
    qkv = project(normed, w_qkv, 32.0)
    owned = deliver(qkv)
    attended = attend_local(owned, k_cache, v_cache, lengths)
    scaled, unit = level(attended)
    out = deliver([jnp.concatenate(project(scaled, w_out, 8.0), axis=-1)])
    return (out.astype(jnp.float32) * unit).astype(jnp.bfloat16)


def solution(mesh):
    return jax.shard_map(
        on_device,
        mesh=mesh,
        in_specs=(
            P(("gx", "gy"), None),
            P(),
            P("gy", "gx"),
            P(("gx", "gy"), None, None),
            P(("gx", "gy"), None, None),
            P(("gx", "gy")),
            P("gy", "gx"),
        ),
        out_specs=P(("gx", "gy"), None),
        check_vma=False,
    )
```

```python
import functools
import math

import jax
import jax.numpy as jnp
from jax import lax
from jax.experimental import pallas as pl
from jax.experimental.pallas import tpu as pltpu
from jax.sharding import PartitionSpec as P

HQ = 128
KVH = 8
HD = 128


eps = 1e-05
theta = 500000.0
ROOM = 50 * 2**20


def rotate(values, position, head_size):
    half = head_size // 2
    index = jnp.arange(half, dtype=jnp.float32)
    freqs = theta ** (-2.0 * index / head_size)
    angle = position[:, None, None] * freqs[None, None, :]
    cosine = jnp.cos(angle)
    sine = jnp.sin(angle)
    first = values[..., :half]
    second = values[..., half:]
    return jnp.concatenate(
        [first * cosine - second * sine, second * cosine + first * sine], axis=-1
    )


PART = 128
GROUP = 4


def attend_kernel(lengths, query, key_new, value_new, k_cache, v_cache, out, keys, values, wide, sems):
    rows, span = keys.shape[:2]
    share = HQ // KVH
    parts = span // PART
    scale = 1.0 / math.sqrt(HD)

    def copy(cache, row, count):
        source, target = ((k_cache, keys), (v_cache, values))[cache]
        some = pl.ds(0, count)
        return pltpu.make_async_copy(
            source.at[row, some], target.at[row, some], sems.at[row, cache]
        )

    def by_length(length, act):
        for case in range(1, parts + 1):
            pl.when((length + PART - 1) // PART == case)(functools.partial(act, case * PART))

    def start(cache, row):
        by_length(lengths[row], lambda count: copy(cache, row, count).start())

    def wait(cache, row):
        by_length(lengths[row], lambda count: copy(cache, row, count).wait())

    def clear(row, part):
        values[row, part * PART : (part + 1) * PART] = jnp.zeros(
            (PART, values.shape[2]), values.dtype
        )

    def score(row, wide, count):
        for group in range(KVH):
            heads = pl.ds(group * share, share)
            side = group % 2 * HD
            wide[heads, side : side + HD] = query[row, heads]
        scores = [
            lax.dot_general(
                wide[2 * share * pair : 2 * share * (pair + 1)],
                keys[row, :count, 2 * HD * pair : 2 * HD * (pair + 1)],
                (((1,), (1,)), ((), ())),
                preferred_element_type=jnp.float32,
            )
            for pair in range(KVH // 2)
        ]
        scores = jnp.concatenate(scores, axis=0)
        position = lax.broadcasted_iota(jnp.int32, scores.shape, 1)
        return jnp.where(position < lengths[row], scores * scale, -jnp.inf)

    def weigh(row, scores):
        fresh_key = jnp.broadcast_to(key_new[row][:, None, :], (KVH, share, HD))
        fresh_key = fresh_key.reshape(HQ, HD).astype(jnp.float32)
        fresh = jnp.sum(query[row].astype(jnp.float32) * fresh_key, axis=1, keepdims=True) * scale
        top = jnp.maximum(jnp.max(scores, axis=1, keepdims=True), fresh)
        probs = jnp.exp(scores - top)
        pnew = jnp.exp(fresh - top)
        unit = 1.0 / (jnp.sum(probs, axis=1, keepdims=True) + pnew)
        weights = (probs * unit).astype(jnp.bfloat16)
        return weights, (pnew * unit).astype(jnp.bfloat16).astype(jnp.float32)

    def mix(row, weights, wnew, count):
        for pair in range(KVH // 2):
            mixed = jnp.dot(
                weights[2 * share * pair : 2 * share * (pair + 1)],
                values[row, :count, 2 * HD * pair : 2 * HD * (pair + 1)],
                preferred_element_type=jnp.float32,
            )
            for side in range(2):
                group = 2 * pair + side
                heads = slice(group * share, (group + 1) * share)
                own = mixed[side * share : (side + 1) * share, side * HD : (side + 1) * HD]
                own = own + wnew[heads] * value_new[row, group : group + 1]
                out[row, heads] = own.astype(out.dtype)

    def group(row, count):
        each = [row + at for at in range(GROUP)]
        for one in each:
            wait(0, one)
            for part in range(1, count // PART):
                pl.when(lengths[one] <= part * PART)(functools.partial(clear, one, part))
        scores = [score(one, wide.at[at], count) for at, one in enumerate(each)]
        weighed = [weigh(one, of_one) for one, of_one in zip(each, scores)]
        for one in each:
            wait(1, one)
        for one, (weights, wnew) in zip(each, weighed):
            mix(one, weights, wnew, count)

    @pl.loop(0, rows // GROUP)
    def _(index):
        for cache in range(2):

            @pl.loop(0, GROUP)
            def _(at):
                start(cache, index * GROUP + at)

    wide[...] = jnp.zeros_like(wide)

    @pl.loop(0, rows // GROUP)
    def _(index):
        row = index * GROUP
        longest = lengths[row]
        for at in range(1, GROUP):
            longest = jnp.maximum(longest, lengths[row + at])
        by_length(longest, functools.partial(group, row))


def attend_local(owned, k_cache, v_cache, lengths):
    rows = owned.shape[0]
    query = owned[:, : HQ * HD].reshape(rows, HQ, HD).astype(jnp.float32)
    key_new = owned[:, HQ * HD : (HQ + KVH) * HD].reshape(rows, KVH, HD).astype(jnp.float32)
    value_new = owned[:, (HQ + KVH) * HD :].reshape(rows, KVH, HD).astype(jnp.float32)
    position = lengths.astype(jnp.float32)
    query = rotate(query, position, HD).astype(jnp.bfloat16)
    key_new = rotate(key_new, position, HD).astype(jnp.bfloat16)
    span, width = k_cache.shape[1:]
    vmem = pl.BlockSpec(memory_space=pltpu.VMEM)
    anywhere = pl.BlockSpec(memory_space=pl.ANY)
    mixed = pl.pallas_call(
        attend_kernel,
        in_specs=[
            pl.BlockSpec(memory_space=pltpu.SMEM),
            vmem,
            vmem,
            vmem,
            anywhere,
            anywhere,
        ],
        out_specs=vmem,
        out_shape=jax.ShapeDtypeStruct((rows, HQ, HD), jnp.bfloat16),
        scratch_shapes=[
            pltpu.VMEM((rows, span, width), jnp.bfloat16),
            pltpu.VMEM((rows, span, width), jnp.bfloat16),
            pltpu.VMEM((GROUP, HQ, 2 * HD), jnp.bfloat16),
            pltpu.SemaphoreType.DMA((rows, 2)),
        ],
        compiler_params=pltpu.CompilerParams(vmem_limit_bytes=ROOM),
        cost_estimate=pl.CostEstimate(
            flops=4 * rows * span * width * HQ,
            bytes_accessed=2 * rows * span * width,
            transcendentals=rows * span * HQ,
        ),
    )(lengths, query, key_new, value_new, k_cache, v_cache)
    return mixed.reshape(rows, HQ * HD)


def swap(block, axis, bit):
    count = lax.axis_size(axis)
    return lax.ppermute(block, axis, [(i, i ^ bit) for i in range(count)])


def all_rows(block):
    if lax.axis_size("gx") != 8:
        pieces = lax.all_gather(block, "gx", axis=0)
        count, rows, width = pieces.shape
        return pieces.reshape(count, 2, rows // 2, width).transpose(1, 0, 2, 3)
    mine = [block] + [swap(block, "gx", chip) for chip in (2, 4, 6)]
    theirs = [swap(piece, "gx", 1) for piece in mine]
    pieces = [piece for pair in zip(mine, theirs) for piece in pair]
    halves = [piece.reshape(2, 1, -1, block.shape[1]) for piece in pieces]
    return jnp.concatenate(halves, axis=1)


def multiply_kernel(start, far, near, weights, out, held, sems):
    parts, depth, columns = held.shape

    def copy(part):
        return pltpu.make_async_copy(
            weights.at[pl.ds(part * depth, depth), pl.ds(start, columns)],
            held.at[part],
            sems.at[part],
        )

    def product(part):
        copy(part).wait()
        some = pl.ds(part * depth, depth)
        rows = jnp.concatenate([far[:, some], near[:, some]], axis=0)
        return jnp.dot(rows, held[part], preferred_element_type=jnp.float32)

    for part in range(parts):
        copy(part).start()
    out[...] = product(0)

    @pl.loop(1, parts)
    def _(part):
        out[...] += product(part)


def multiply(far, near, weights, start, columns):
    half, width = far.shape
    depth = 1024
    vmem = pl.BlockSpec(memory_space=pltpu.VMEM)
    return pl.pallas_call(
        functools.partial(multiply_kernel, start),
        in_specs=[vmem, vmem, pl.BlockSpec(memory_space=pl.ANY)],
        out_specs=vmem,
        out_shape=jax.ShapeDtypeStruct((2 * half, columns), jnp.float32),
        scratch_shapes=[
            pltpu.VMEM((width // depth, depth, columns), jnp.bfloat16),
            pltpu.SemaphoreType.DMA((width // depth,)),
        ],
        compiler_params=pltpu.CompilerParams(vmem_limit_bytes=ROOM),
        cost_estimate=pl.CostEstimate(
            flops=4 * half * width * columns,
            bytes_accessed=2 * width * columns,
            transcendentals=0,
        ),
    )(far, near, weights)


def project(rows, weights, scale):
    width, columns = weights.shape
    here = lax.axis_index("gy")

    def features(owner):
        return lax.dynamic_slice_in_dim(rows, owner * width, width, axis=1)

    def pack(values):
        return (values * scale).astype(jnp.float16)

    def send(packed, bit):
        return swap(packed, "gy", bit).astype(jnp.float32) * (1.0 / scale)

    near, far, last = (swap(features(here ^ bit), "gy", bit) for bit in (1, 2, 3))
    near = jnp.concatenate([features(here), near])
    far = all_rows(jnp.concatenate([far, last]))
    near = all_rows(near)
    shape = (2, 2) + far.shape[1:3]
    far = far.reshape(-1, width)
    near = near.reshape(-1, width)
    first = columns // 512 * 256 if columns % 256 == 0 else columns
    left = multiply(far, near, weights, 0, first).reshape(shape + (first,))
    go_left = pack(left[:, 1])
    go_left, far, near = lax.optimization_barrier((go_left, far, near))
    left = left[:, 0] + send(go_left, 1)
    if first == columns:
        return [left[1] + send(pack(left[0]), 2)]
    right = multiply(far, near, weights, first, columns - first)
    right = right.reshape(shape + (columns - first,))
    go_far = pack(right[0, 1])
    across, go_near = lax.optimization_barrier((pack(left[0]), pack(right[1, 1])))
    left = left[1] + send(across, 2)
    across = pack(right[0, 0] + send(go_far, 1))
    right = right[1, 0] + send(go_near, 1) + send(across, 2)
    return [left, right]


def collect(columns):
    columns = columns.astype(jnp.bfloat16)
    count, rows, width = columns.shape
    if count != 8:
        return lax.all_to_all(columns, "gx", split_axis=0, concat_axis=0)
    pairs = [columns[:2]] + [
        swap(columns[chip : chip + 2], "gx", chip) for chip in (2, 4, 6)
    ]
    theirs = swap(jnp.stack([pair[1] for pair in pairs]), "gx", 1)
    owned = jnp.stack([pair[0] for pair in pairs])
    return jnp.stack([owned, theirs], axis=1).reshape(count, rows, width)


def deliver(parts):
    owned = jnp.concatenate([collect(part) for part in parts], axis=-1)
    count, rows, width = owned.shape
    if count != 8:
        return owned.transpose(1, 0, 2).reshape(rows, count * width)
    me = lax.axis_index("gx")
    blocks = [lax.dynamic_index_in_dim(owned, at ^ me, keepdims=False) for at in range(count)]
    return jnp.concatenate(blocks, axis=1)


def level(rows):
    rows = rows.astype(jnp.float32)
    top = jnp.max(jnp.abs(rows), axis=-1, keepdims=True)
    scale = jnp.ones_like(top)
    unit = jnp.ones_like(top)
    for power in (64, 32, 16, 8, 4, 2, 1):
        large = top * scale > 2.0 ** (power - 1)
        scale = jnp.where(large, scale * 2.0**-power, scale)
        unit = jnp.where(large, unit * 2.0**power, unit)
    for power in (64, 32, 16, 8, 4, 2, 1):
        small = top * scale <= 2.0**-power
        scale = jnp.where(small, scale * 2.0**power, scale)
        unit = jnp.where(small, unit * 2.0**-power, unit)
    return (rows * scale).astype(jnp.bfloat16), unit


def on_device(hidden_in, norm_gain, w_qkv, k_cache, v_cache, lengths, w_out):
    widened = hidden_in.astype(jnp.float32)
    normed = (
        widened * lax.rsqrt(jnp.mean(widened * widened, axis=-1, keepdims=True) + eps) * norm_gain
    ).astype(jnp.bfloat16)
    qkv = project(normed, w_qkv, 32.0)
    owned = deliver(qkv)
    attended = attend_local(owned, k_cache, v_cache, lengths)
    scaled, unit = level(attended)
    out = deliver([jnp.concatenate(project(scaled, w_out, 8.0), axis=-1)])
    return (out.astype(jnp.float32) * unit).astype(jnp.bfloat16)


def solution(mesh):
    return jax.shard_map(
        on_device,
        mesh=mesh,
        in_specs=(
            P(("gx", "gy"), None),
            P(),
            P("gy", "gx"),
            P(("gx", "gy"), None, None),
            P(("gx", "gy"), None, None),
            P(("gx", "gy")),
            P("gy", "gx"),
        ),
        out_specs=P(("gx", "gy"), None),
        check_vma=False,
    )
```

```python
import functools
import math

import jax
import jax.numpy as jnp
from jax import lax
from jax.experimental import pallas as pl
from jax.experimental.pallas import tpu as pltpu
from jax.sharding import PartitionSpec as P

HQ = 128
KVH = 8
HD = 128


eps = 1e-05
theta = 500000.0
ROOM = 47 * 2**20


def rotate(values, position, head_size):
    half = head_size // 2
    index = jnp.arange(half, dtype=jnp.float32)
    freqs = theta ** (-2.0 * index / head_size)
    angle = position[:, None, None] * freqs[None, None, :]
    cosine = jnp.cos(angle)
    sine = jnp.sin(angle)
    first = values[..., :half]
    second = values[..., half:]
    return jnp.concatenate(
        [first * cosine - second * sine, second * cosine + first * sine], axis=-1
    )


PART = 128
DEPTH = 1024
GROUP = 4


def attend_kernel(lengths, query, key_new, value_new, k_cache, v_cache, out, keys, values, wide, sems):
    rows, span = keys.shape[:2]
    share = HQ // KVH
    parts = span // PART
    scale = 1.0 / math.sqrt(HD)

    def copy(cache, row, count):
        source, target = ((k_cache, keys), (v_cache, values))[cache]
        some = pl.ds(0, count)
        return pltpu.make_async_copy(
            source.at[row, some], target.at[row, some], sems.at[row, cache]
        )

    def by_length(length, act):
        for case in range(1, parts + 1):
            pl.when((length + PART - 1) // PART == case)(functools.partial(act, case * PART))

    def start(cache, row):
        by_length(lengths[row], lambda count: copy(cache, row, count).start())

    def wait(cache, row):
        by_length(lengths[row], lambda count: copy(cache, row, count).wait())

    def clear(row, part):
        values[row, part * PART : (part + 1) * PART] = jnp.zeros(
            (PART, values.shape[2]), values.dtype
        )

    def score(row, wide, count):
        for group in range(KVH):
            heads = pl.ds(group * share, share)
            side = group % 2 * HD
            wide[heads, side : side + HD] = query[row, heads]
        scores = [
            lax.dot_general(
                wide[2 * share * pair : 2 * share * (pair + 1)],
                keys[row, :count, 2 * HD * pair : 2 * HD * (pair + 1)],
                (((1,), (1,)), ((), ())),
                preferred_element_type=jnp.float32,
            )
            for pair in range(KVH // 2)
        ]
        scores = jnp.concatenate(scores, axis=0)
        position = lax.broadcasted_iota(jnp.int32, scores.shape, 1)
        return jnp.where(position < lengths[row], scores * scale, -jnp.inf)

    def weigh(row, scores):
        fresh_key = jnp.broadcast_to(key_new[row][:, None, :], (KVH, share, HD))
        fresh_key = fresh_key.reshape(HQ, HD).astype(jnp.float32)
        fresh = jnp.sum(query[row].astype(jnp.float32) * fresh_key, axis=1, keepdims=True) * scale
        top = jnp.maximum(jnp.max(scores, axis=1, keepdims=True), fresh)
        probs = jnp.exp(scores - top)
        pnew = jnp.exp(fresh - top)
        unit = 1.0 / (jnp.sum(probs, axis=1, keepdims=True) + pnew)
        weights = (probs * unit).astype(jnp.bfloat16)
        return weights, (pnew * unit).astype(jnp.bfloat16).astype(jnp.float32)

    def mix(row, weights, wnew, count):
        for pair in range(KVH // 2):
            mixed = jnp.dot(
                weights[2 * share * pair : 2 * share * (pair + 1)],
                values[row, :count, 2 * HD * pair : 2 * HD * (pair + 1)],
                preferred_element_type=jnp.float32,
            )
            for side in range(2):
                group = 2 * pair + side
                heads = slice(group * share, (group + 1) * share)
                own = mixed[side * share : (side + 1) * share, side * HD : (side + 1) * HD]
                own = own + wnew[heads] * value_new[row, group : group + 1]
                out[row, heads] = own.astype(out.dtype)

    def group(row, count):
        each = [row + at for at in range(GROUP)]
        for one in each:
            wait(0, one)
            for part in range(1, count // PART):
                pl.when(lengths[one] <= part * PART)(functools.partial(clear, one, part))
        scores = [score(one, wide.at[at], count) for at, one in enumerate(each)]
        weighed = [weigh(one, of_one) for one, of_one in zip(each, scores)]
        for one in each:
            wait(1, one)
        for one, (weights, wnew) in zip(each, weighed):
            mix(one, weights, wnew, count)

    @pl.loop(0, rows // GROUP)
    def _(index):
        for cache in range(2):

            @pl.loop(0, GROUP)
            def _(at):
                start(cache, index * GROUP + at)

    wide[...] = jnp.zeros_like(wide)

    @pl.loop(0, rows // GROUP)
    def _(index):
        row = index * GROUP
        longest = lengths[row]
        for at in range(1, GROUP):
            longest = jnp.maximum(longest, lengths[row + at])
        by_length(longest, functools.partial(group, row))


def attend_local(owned, k_cache, v_cache, lengths):
    rows = owned.shape[0]
    query = owned[:, : HQ * HD].reshape(rows, HQ, HD).astype(jnp.float32)
    key_new = owned[:, HQ * HD : (HQ + KVH) * HD].reshape(rows, KVH, HD).astype(jnp.float32)
    value_new = owned[:, (HQ + KVH) * HD :].reshape(rows, KVH, HD).astype(jnp.float32)
    position = lengths.astype(jnp.float32)
    query = rotate(query, position, HD).astype(jnp.bfloat16)
    key_new = rotate(key_new, position, HD).astype(jnp.bfloat16)
    span, width = k_cache.shape[1:]
    vmem = pl.BlockSpec(memory_space=pltpu.VMEM)
    anywhere = pl.BlockSpec(memory_space=pl.ANY)
    mixed = pl.pallas_call(
        attend_kernel,
        in_specs=[
            pl.BlockSpec(memory_space=pltpu.SMEM),
            vmem,
            vmem,
            vmem,
            anywhere,
            anywhere,
        ],
        out_specs=vmem,
        out_shape=jax.ShapeDtypeStruct((rows, HQ, HD), jnp.bfloat16),
        scratch_shapes=[
            pltpu.VMEM((rows, span, width), jnp.bfloat16),
            pltpu.VMEM((rows, span, width), jnp.bfloat16),
            pltpu.VMEM((GROUP, HQ, 2 * HD), jnp.bfloat16),
            pltpu.SemaphoreType.DMA((rows, 2)),
        ],
        compiler_params=pltpu.CompilerParams(vmem_limit_bytes=ROOM),
        cost_estimate=pl.CostEstimate(
            flops=4 * rows * span * width * HQ,
            bytes_accessed=2 * rows * span * width,
            transcendentals=rows * span * HQ,
        ),
    )(lengths, query, key_new, value_new, k_cache, v_cache)
    return mixed.reshape(rows, HQ * HD)


def swap(block, axis, bit):
    count = lax.axis_size(axis)
    return lax.ppermute(block, axis, [(i, i ^ bit) for i in range(count)])


def all_rows(block, also=None):
    if lax.axis_size("gx") != 8:
        pieces = lax.all_gather(block, "gx", axis=0)
        count, rows, width = pieces.shape
        return pieces.reshape(count, 2, rows // 2, width).transpose(1, 0, 2, 3), also
    mine = [block] + [swap(block, "gx", chip) for chip in (2, 4, 6)]
    if also is not None:
        mine[1], also = lax.optimization_barrier((mine[1], also))
    theirs = [swap(piece, "gx", 1) for piece in mine]
    pieces = [piece for pair in zip(mine, theirs) for piece in pair]
    halves = [piece.reshape(2, 1, -1, block.shape[1]) for piece in pieces]
    return jnp.concatenate(halves, axis=1), also


def multiply_kernel(start, far, near, head, weights, out, held, sems):
    parts, depth, columns = held.shape
    ready = 1 if head.shape[0] == depth else 0

    def copy(part):
        return pltpu.make_async_copy(
            weights.at[pl.ds(part * depth, depth), pl.ds(start, columns)],
            held.at[part],
            sems.at[part],
        )

    def product(part, block):
        some = pl.ds(part * depth, depth)
        rows = jnp.concatenate([far[:, some], near[:, some]], axis=0)
        return jnp.dot(rows, block, preferred_element_type=jnp.float32)

    for part in range(ready, parts):
        copy(part).start()
    if ready:
        out[...] = product(0, head[...])
    else:
        copy(0).wait()
        out[...] = product(0, held[0])

    @pl.loop(1, parts)
    def _(part):
        copy(part).wait()
        out[...] += product(part, held[part])


def multiply(far, near, head, weights, start, columns):
    half, width = far.shape
    depth = DEPTH
    vmem = pl.BlockSpec(memory_space=pltpu.VMEM)
    return pl.pallas_call(
        functools.partial(multiply_kernel, start),
        in_specs=[vmem, vmem, vmem, pl.BlockSpec(memory_space=pl.ANY)],
        out_specs=vmem,
        out_shape=jax.ShapeDtypeStruct((2 * half, columns), jnp.float32),
        scratch_shapes=[
            pltpu.VMEM((width // depth, depth, columns), jnp.bfloat16),
            pltpu.SemaphoreType.DMA((width // depth,)),
        ],
        compiler_params=pltpu.CompilerParams(vmem_limit_bytes=ROOM),
        cost_estimate=pl.CostEstimate(
            flops=4 * half * width * columns,
            bytes_accessed=2 * width * columns,
            transcendentals=0,
        ),
    )(far, near, head, weights)


def project(rows, weights, scale):
    width, columns = weights.shape
    here = lax.axis_index("gy")

    def features(owner):
        return lax.dynamic_slice_in_dim(rows, owner * width, width, axis=1)

    def pack(values):
        return (values * scale).astype(jnp.float16)

    def send(packed, bit):
        return swap(packed, "gy", bit).astype(jnp.float32) * (1.0 / scale)

    near, far, last = (swap(features(here ^ bit), "gy", bit) for bit in (1, 2, 3))
    near = jnp.concatenate([features(here), near])
    first = columns // 512 * 256 if columns % 256 == 0 else columns
    head = weights[:DEPTH, :first]
    none = jnp.zeros((16, 128), weights.dtype)
    far = all_rows(jnp.concatenate([far, last]))[0]
    near, head = all_rows(near, head)
    shape = (2, 2) + far.shape[1:3]
    far = far.reshape(-1, width)
    near = near.reshape(-1, width)
    left = multiply(far, near, head, weights, 0, first).reshape(shape + (first,))
    go_left = pack(left[:, 1])
    go_left, far, near = lax.optimization_barrier((go_left, far, near))
    left = left[:, 0] + send(go_left, 1)
    if first == columns:
        return [left[1] + send(pack(left[0]), 2)]
    right = multiply(far, near, none, weights, first, columns - first)
    right = right.reshape(shape + (columns - first,))
    go_far = pack(right[0, 1])
    across, go_near = lax.optimization_barrier((pack(left[0]), pack(right[1, 1])))
    left = left[1] + send(across, 2)
    across = pack(right[0, 0] + send(go_far, 1))
    right = right[1, 0] + send(go_near, 1) + send(across, 2)
    return [left, right]


def collect(columns):
    columns = columns.astype(jnp.bfloat16)
    count, rows, width = columns.shape
    if count != 8:
        return lax.all_to_all(columns, "gx", split_axis=0, concat_axis=0)
    pairs = [columns[:2]] + [
        swap(columns[chip : chip + 2], "gx", chip) for chip in (2, 4, 6)
    ]
    theirs = swap(jnp.stack([pair[1] for pair in pairs]), "gx", 1)
    owned = jnp.stack([pair[0] for pair in pairs])
    return jnp.stack([owned, theirs], axis=1).reshape(count, rows, width)


def deliver(parts):
    owned = jnp.concatenate([collect(part) for part in parts], axis=-1)
    count, rows, width = owned.shape
    if count != 8:
        return owned.transpose(1, 0, 2).reshape(rows, count * width)
    me = lax.axis_index("gx")
    blocks = [lax.dynamic_index_in_dim(owned, at ^ me, keepdims=False) for at in range(count)]
    return jnp.concatenate(blocks, axis=1)


def level(rows):
    rows = rows.astype(jnp.float32)
    top = jnp.max(jnp.abs(rows), axis=-1, keepdims=True)
    scale = jnp.ones_like(top)
    unit = jnp.ones_like(top)
    for power in (64, 32, 16, 8, 4, 2, 1):
        large = top * scale > 2.0 ** (power - 1)
        scale = jnp.where(large, scale * 2.0**-power, scale)
        unit = jnp.where(large, unit * 2.0**power, unit)
    for power in (64, 32, 16, 8, 4, 2, 1):
        small = top * scale <= 2.0**-power
        scale = jnp.where(small, scale * 2.0**power, scale)
        unit = jnp.where(small, unit * 2.0**-power, unit)
    return (rows * scale).astype(jnp.bfloat16), unit


def on_device(hidden_in, norm_gain, w_qkv, k_cache, v_cache, lengths, w_out):
    widened = hidden_in.astype(jnp.float32)
    normed = (
        widened * lax.rsqrt(jnp.mean(widened * widened, axis=-1, keepdims=True) + eps) * norm_gain
    ).astype(jnp.bfloat16)
    qkv = project(normed, w_qkv, 32.0)
    owned = deliver(qkv)
    attended = attend_local(owned, k_cache, v_cache, lengths)
    scaled, unit = level(attended)
    out = deliver([jnp.concatenate(project(scaled, w_out, 8.0), axis=-1)])
    return (out.astype(jnp.float32) * unit).astype(jnp.bfloat16)


def solution(mesh):
    return jax.shard_map(
        on_device,
        mesh=mesh,
        in_specs=(
            P(("gx", "gy"), None),
            P(),
            P("gy", "gx"),
            P(("gx", "gy"), None, None),
            P(("gx", "gy"), None, None),
            P(("gx", "gy")),
            P("gy", "gx"),
        ),
        out_specs=P(("gx", "gy"), None),
        check_vma=False,
    )
```

```python
import functools
import math

import jax
import jax.numpy as jnp
from jax import lax
from jax.experimental import pallas as pl
from jax.experimental.pallas import tpu as pltpu
from jax.sharding import PartitionSpec as P

HQ = 128
KVH = 8
HD = 128


eps = 1e-05
theta = 500000.0
ROOM = 50 * 2**20


def rotate(values, position, head_size):
    half = head_size // 2
    index = jnp.arange(half, dtype=jnp.float32)
    freqs = theta ** (-2.0 * index / head_size)
    angle = position[:, None, None] * freqs[None, None, :]
    cosine = jnp.cos(angle)
    sine = jnp.sin(angle)
    first = values[..., :half]
    second = values[..., half:]
    return jnp.concatenate(
        [first * cosine - second * sine, second * cosine + first * sine], axis=-1
    )


PART = 128
GROUP = 4


def attend_kernel(lengths, query, key_new, value_new, k_cache, v_cache, out, keys, values, wide, sems):
    rows, span = keys.shape[:2]
    share = HQ // KVH
    parts = span // PART
    scale = 1.0 / math.sqrt(HD)

    def copy(cache, row, count):
        source, target = ((k_cache, keys), (v_cache, values))[cache]
        some = pl.ds(0, count)
        return pltpu.make_async_copy(
            source.at[row, some], target.at[row, some], sems.at[row, cache]
        )

    def by_length(length, act):
        for case in range(1, parts + 1):
            pl.when((length + PART - 1) // PART == case)(functools.partial(act, case * PART))

    def start(cache, row):
        by_length(lengths[row], lambda count: copy(cache, row, count).start())

    def wait(cache, row):
        by_length(lengths[row], lambda count: copy(cache, row, count).wait())

    def clear(row, part):
        values[row, part * PART : (part + 1) * PART] = jnp.zeros(
            (PART, values.shape[2]), values.dtype
        )

    def score(row, wide, count):
        for group in range(KVH):
            heads = pl.ds(group * share, share)
            side = group % 2 * HD
            wide[heads, side : side + HD] = query[row, heads]
        scores = [
            lax.dot_general(
                wide[2 * share * pair : 2 * share * (pair + 1)],
                keys[row, :count, 2 * HD * pair : 2 * HD * (pair + 1)],
                (((1,), (1,)), ((), ())),
                preferred_element_type=jnp.float32,
            )
            for pair in range(KVH // 2)
        ]
        scores = jnp.concatenate(scores, axis=0)
        position = lax.broadcasted_iota(jnp.int32, scores.shape, 1)
        return jnp.where(position < lengths[row], scores * scale, -jnp.inf)

    def weigh(row, scores):
        fresh_key = jnp.broadcast_to(key_new[row][:, None, :], (KVH, share, HD))
        fresh_key = fresh_key.reshape(HQ, HD).astype(jnp.float32)
        fresh = jnp.sum(query[row].astype(jnp.float32) * fresh_key, axis=1, keepdims=True) * scale
        top = jnp.maximum(jnp.max(scores, axis=1, keepdims=True), fresh)
        probs = jnp.exp(scores - top)
        pnew = jnp.exp(fresh - top)
        unit = 1.0 / (jnp.sum(probs, axis=1, keepdims=True) + pnew)
        weights = (probs * unit).astype(jnp.bfloat16)
        return weights, (pnew * unit).astype(jnp.bfloat16).astype(jnp.float32)

    def mix(row, weights, wnew, count):
        for pair in range(KVH // 2):
            mixed = jnp.dot(
                weights[2 * share * pair : 2 * share * (pair + 1)],
                values[row, :count, 2 * HD * pair : 2 * HD * (pair + 1)],
                preferred_element_type=jnp.float32,
            )
            for side in range(2):
                group = 2 * pair + side
                heads = slice(group * share, (group + 1) * share)
                own = mixed[side * share : (side + 1) * share, side * HD : (side + 1) * HD]
                own = own + wnew[heads] * value_new[row, group : group + 1]
                out[row, heads] = own.astype(out.dtype)

    def group(row, count):
        each = [row + at for at in range(GROUP)]
        for one in each:
            wait(0, one)
            for part in range(1, count // PART):
                pl.when(lengths[one] <= part * PART)(functools.partial(clear, one, part))
        scores = [score(one, wide.at[at], count) for at, one in enumerate(each)]
        weighed = [weigh(one, of_one) for one, of_one in zip(each, scores)]
        for one in each:
            wait(1, one)
        for one, (weights, wnew) in zip(each, weighed):
            mix(one, weights, wnew, count)

    @pl.loop(0, rows // GROUP)
    def _(index):
        for cache in range(2):

            @pl.loop(0, GROUP)
            def _(at):
                start(cache, index * GROUP + at)

    wide[...] = jnp.zeros_like(wide)

    @pl.loop(0, rows // GROUP)
    def _(index):
        row = index * GROUP
        longest = lengths[row]
        for at in range(1, GROUP):
            longest = jnp.maximum(longest, lengths[row + at])
        by_length(longest, functools.partial(group, row))


def attend_local(owned, k_cache, v_cache, lengths):
    rows = owned.shape[0]
    query = owned[:, : HQ * HD].reshape(rows, HQ, HD).astype(jnp.float32)
    key_new = owned[:, HQ * HD : (HQ + KVH) * HD].reshape(rows, KVH, HD).astype(jnp.float32)
    value_new = owned[:, (HQ + KVH) * HD :].reshape(rows, KVH, HD).astype(jnp.float32)
    position = lengths.astype(jnp.float32)
    query = rotate(query, position, HD).astype(jnp.bfloat16)
    key_new = rotate(key_new, position, HD).astype(jnp.bfloat16)
    span, width = k_cache.shape[1:]
    vmem = pl.BlockSpec(memory_space=pltpu.VMEM)
    anywhere = pl.BlockSpec(memory_space=pl.ANY)
    mixed = pl.pallas_call(
        attend_kernel,
        in_specs=[
            pl.BlockSpec(memory_space=pltpu.SMEM),
            vmem,
            vmem,
            vmem,
            anywhere,
            anywhere,
        ],
        out_specs=vmem,
        out_shape=jax.ShapeDtypeStruct((rows, HQ, HD), jnp.bfloat16),
        scratch_shapes=[
            pltpu.VMEM((rows, span, width), jnp.bfloat16),
            pltpu.VMEM((rows, span, width), jnp.bfloat16),
            pltpu.VMEM((GROUP, HQ, 2 * HD), jnp.bfloat16),
            pltpu.SemaphoreType.DMA((rows, 2)),
        ],
        compiler_params=pltpu.CompilerParams(vmem_limit_bytes=ROOM),
        cost_estimate=pl.CostEstimate(
            flops=4 * rows * span * width * HQ,
            bytes_accessed=2 * rows * span * width,
            transcendentals=rows * span * HQ,
        ),
    )(lengths, query, key_new, value_new, k_cache, v_cache)
    return mixed.reshape(rows, HQ * HD)


def swap(block, axis, bit):
    count = lax.axis_size(axis)
    return lax.ppermute(block, axis, [(i, i ^ bit) for i in range(count)])


def all_rows(block):
    if lax.axis_size("gx") != 8:
        pieces = lax.all_gather(block, "gx", axis=0)
        count, rows, width = pieces.shape
        return pieces.reshape(count, 2, rows // 2, width).transpose(1, 0, 2, 3)
    mine = [block] + [swap(block, "gx", chip) for chip in (2, 4, 6)]
    theirs = [swap(piece, "gx", 1) for piece in mine]
    pieces = [piece for pair in zip(mine, theirs) for piece in pair]
    halves = [piece.reshape(2, 1, -1, block.shape[1]) for piece in pieces]
    return jnp.concatenate(halves, axis=1)


def multiply_kernel(start, depth, far, near, weights, out, held, sems):
    width, columns = held.shape
    parts = width // depth
    half = depth // 2

    def copy(at, count, sem):
        some = pl.ds(at, count)
        return pltpu.make_async_copy(
            weights.at[some, pl.ds(start, columns)], held.at[some], sems.at[sem]
        )

    def product(at, count, sem):
        copy(at, count, sem).wait()
        some = pl.ds(at, count)
        rows = jnp.concatenate([far[:, some], near[:, some]], axis=0)
        return jnp.dot(rows, held[some], preferred_element_type=jnp.float32)

    copy(0, half, 0).start()
    copy(half, half, parts).start()
    for part in range(1, parts):
        copy(part * depth, depth, part).start()
    out[...] = product(0, half, 0)
    out[...] += product(half, half, parts)

    @pl.loop(1, parts)
    def _(part):
        out[...] += product(pl.multiple_of(part * depth, depth), depth, part)


def multiply(far, near, weights, start, columns):
    half, width = far.shape
    depth = 1024
    vmem = pl.BlockSpec(memory_space=pltpu.VMEM)
    return pl.pallas_call(
        functools.partial(multiply_kernel, start, depth),
        in_specs=[vmem, vmem, pl.BlockSpec(memory_space=pl.ANY)],
        out_specs=vmem,
        out_shape=jax.ShapeDtypeStruct((2 * half, columns), jnp.float32),
        scratch_shapes=[
            pltpu.VMEM((width, columns), jnp.bfloat16),
            pltpu.SemaphoreType.DMA((width // depth + 1,)),
        ],
        compiler_params=pltpu.CompilerParams(vmem_limit_bytes=ROOM),
        cost_estimate=pl.CostEstimate(
            flops=4 * half * width * columns,
            bytes_accessed=2 * width * columns,
            transcendentals=0,
        ),
    )(far, near, weights)


def project(rows, weights, scale):
    width, columns = weights.shape
    here = lax.axis_index("gy")

    def features(owner):
        return lax.dynamic_slice_in_dim(rows, owner * width, width, axis=1)

    def pack(values):
        return (values * scale).astype(jnp.float16)

    def send(packed, bit):
        return swap(packed, "gy", bit).astype(jnp.float32) * (1.0 / scale)

    near, far, last = (swap(features(here ^ bit), "gy", bit) for bit in (1, 2, 3))
    near = jnp.concatenate([features(here), near])
    far = all_rows(jnp.concatenate([far, last]))
    near = all_rows(near)
    shape = (2, 2) + far.shape[1:3]
    far = far.reshape(-1, width)
    near = near.reshape(-1, width)
    first = columns // 512 * 256 if columns % 256 == 0 else columns
    left = multiply(far, near, weights, 0, first).reshape(shape + (first,))
    go_left = pack(left[:, 1])
    go_left, far, near = lax.optimization_barrier((go_left, far, near))
    left = left[:, 0] + send(go_left, 1)
    if first == columns:
        return [left[1] + send(pack(left[0]), 2)]
    right = multiply(far, near, weights, first, columns - first)
    right = right.reshape(shape + (columns - first,))
    go_far = pack(right[0, 1])
    across, go_near = lax.optimization_barrier((pack(left[0]), pack(right[1, 1])))
    left = left[1] + send(across, 2)
    across = pack(right[0, 0] + send(go_far, 1))
    right = right[1, 0] + send(go_near, 1) + send(across, 2)
    return [left, right]


def collect(columns):
    columns = columns.astype(jnp.bfloat16)
    count, rows, width = columns.shape
    if count != 8:
        return lax.all_to_all(columns, "gx", split_axis=0, concat_axis=0)
    pairs = [columns[:2]] + [
        swap(columns[chip : chip + 2], "gx", chip) for chip in (2, 4, 6)
    ]
    theirs = swap(jnp.stack([pair[1] for pair in pairs]), "gx", 1)
    owned = jnp.stack([pair[0] for pair in pairs])
    return jnp.stack([owned, theirs], axis=1).reshape(count, rows, width)


def deliver(parts):
    owned = jnp.concatenate([collect(part) for part in parts], axis=-1)
    count, rows, width = owned.shape
    if count != 8:
        return owned.transpose(1, 0, 2).reshape(rows, count * width)
    me = lax.axis_index("gx")
    blocks = [lax.dynamic_index_in_dim(owned, at ^ me, keepdims=False) for at in range(count)]
    return jnp.concatenate(blocks, axis=1)


def level(rows):
    rows = rows.astype(jnp.float32)
    top = jnp.max(jnp.abs(rows), axis=-1, keepdims=True)
    scale = jnp.ones_like(top)
    unit = jnp.ones_like(top)
    for power in (64, 32, 16, 8, 4, 2, 1):
        large = top * scale > 2.0 ** (power - 1)
        scale = jnp.where(large, scale * 2.0**-power, scale)
        unit = jnp.where(large, unit * 2.0**power, unit)
    for power in (64, 32, 16, 8, 4, 2, 1):
        small = top * scale <= 2.0**-power
        scale = jnp.where(small, scale * 2.0**power, scale)
        unit = jnp.where(small, unit * 2.0**-power, unit)
    return (rows * scale).astype(jnp.bfloat16), unit


def on_device(hidden_in, norm_gain, w_qkv, k_cache, v_cache, lengths, w_out):
    widened = hidden_in.astype(jnp.float32)
    normed = (
        widened * lax.rsqrt(jnp.mean(widened * widened, axis=-1, keepdims=True) + eps) * norm_gain
    ).astype(jnp.bfloat16)
    qkv = project(normed, w_qkv, 32.0)
    owned = deliver(qkv)
    attended = attend_local(owned, k_cache, v_cache, lengths)
    scaled, unit = level(attended)
    out = deliver([jnp.concatenate(project(scaled, w_out, 8.0), axis=-1)])
    return (out.astype(jnp.float32) * unit).astype(jnp.bfloat16)


def solution(mesh):
    return jax.shard_map(
        on_device,
        mesh=mesh,
        in_specs=(
            P(("gx", "gy"), None),
            P(),
            P("gy", "gx"),
            P(("gx", "gy"), None, None),
            P(("gx", "gy"), None, None),
            P(("gx", "gy")),
            P("gy", "gx"),
        ),
        out_specs=P(("gx", "gy"), None),
        check_vma=False,
    )
```
